32 devices in a mesh: lat: 8 (over z, core), ch: 4 (over y, x).
Axes of the slice: x: 2, y: 2, z: 4, core: 2. Of those that a mesh axis runs over, the one named last changes fastest.
Arguments:
- fields: bfloat16 [2, 704, 32, 1440], P(None, 'lat', 'ch'), may hold values from -6 to 6
- table: bfloat16 [704, 704, 352], P('lat', 'ch'), may hold values from -1 to 1, as said below
Outputs:
- coefficients: float32 [704, 704, 128], P('lat', 'ch')
The draws below stay inside these ranges and needn't reach their ends.
Inputs may be any that keep to these rules, and one draw needn't show every extreme that they name: table[m, l, k] is zero wherever l < m.
All inputs are finite; a program needn't handle non-finite values.
Results may differ from the reference program's by a relative error of at most 0.005.
Values may be sent and summed in bfloat16 or wider, within the bound.
No kernel may reach another device: no remote copies, remote signals or barrier semaphores. Data moves between devices by JAX's collectives and lax.ppermute only.
A program may use at most 128 MiB of HBM per device.

```python
import math
import jax
import jax.numpy as jnp
from jax import lax

NLAT = 704
NLON = 1440
MODES = 704
CH = 32
BATCH = 2
HALF = 352


def draw_table(key, part):
    values = jax.random.truncated_normal(key, -4.0, 4.0, (MODES, MODES, HALF), jnp.float32) * HALF ** (-0.5)
    degree = jnp.arange(MODES, dtype=jnp.int32)[None, :, None]
    order = jnp.arange(MODES, dtype=jnp.int32)[:, None, None]
    return jnp.where(degree >= order, values, 0.0).astype(jnp.bfloat16)


def block_scale(rng, dims, cuts, smallest, largest):
    level = 1.0
    for dim, blocks in cuts:
        heights = jax.random.uniform(jax.random.fold_in(jax.random.fold_in(rng, 6), dim), (blocks,), jnp.float32, smallest / len(cuts), largest / len(cuts))
        level = level * jnp.repeat(jnp.exp(heights), dims[dim] // blocks).reshape((-1,) + (1,) * (len(dims) - 1 - dim))
    return level


def gaussian(rng, shape, width, limit, pieces=(), kind=jnp.bfloat16):
    values = width * jax.random.normal(rng, shape, jnp.float32)
    if pieces:
        values = values * block_scale(rng, shape, pieces, -0.22, 0.18)
    return jnp.clip(values, -limit, limit).astype(kind)


def setup_inputs(seed: int = 0) -> dict:
    arg_keys = jax.random.split(jax.random.key(seed), 3)
    fields = gaussian(arg_keys[0], (BATCH, NLAT, CH, NLON), 1.0, 6.0, ((1, 8), (2, 4)))
    table = draw_table(jax.random.fold_in(arg_keys[2], 71), 0)
    return dict(fields=fields, table=table)


def fourier_table(nlon, modes):
    cols = jnp.arange(nlon, dtype=jnp.int32)[:, None]
    orders = jnp.arange(modes, dtype=jnp.int32)[None, :]
    phase = (cols * orders % nlon).astype(jnp.float32) * (2.0 * math.pi / nlon)
    factor = 1.0 / math.sqrt(nlon)
    return jnp.concatenate([jnp.cos(phase) * factor, -jnp.sin(phase) * factor], axis=1).astype(jnp.bfloat16)

def reference(fields, table):
    fourier = fourier_table(NLON, MODES)

    def transform(sample):
        flat = sample.reshape(NLAT * CH, NLON)
        return jnp.dot(flat, fourier, preferred_element_type=jnp.float32).astype(jnp.bfloat16).reshape(NLAT, CH, 2, MODES)
    spectrum = lax.map(transform, fields)
    north = spectrum[:, :HALF].astype(jnp.float32)
    south = spectrum[:, HALF:][:, ::-1].astype(jnp.float32)
    parts = jnp.concatenate([(north + south).astype(jnp.bfloat16), (north - south).astype(jnp.bfloat16)], axis=1)
    per_order = jnp.transpose(parts, (4, 1, 0, 2, 3)).reshape(MODES, NLAT, BATCH * CH * 2)
    degrees = jnp.arange(MODES, dtype=jnp.int32)[:, None]

    def one_order(items):
        tab_m, par_m, order = items
        even = (degrees - order) % 2 == 0
        zero = jnp.zeros_like(tab_m)
        doubled = jnp.concatenate([jnp.where(even, tab_m, zero), jnp.where(even, zero, tab_m)], axis=1)
        return jnp.dot(doubled, par_m, preferred_element_type=jnp.float32)
    return lax.map(one_order, (table, per_order, jnp.arange(MODES, dtype=jnp.int32)))
```

```python
import functools
import math

import jax
import jax.numpy as jnp
import ml_dtypes
import numpy as np
from jax import lax
from jax.experimental import pallas as pl
from jax.experimental.pallas import tpu as pltpu
from jax.sharding import PartitionSpec as P

LANES = 128
VMEM_LIMIT = 56 * 1024 * 1024
NT = (((1,), (1,)), ((), ()))


def fourier_rows(nlon, slabs, slab, chunk):
    first, count = chunk
    orders = (np.arange(slabs)[:, None] * slab + first + np.arange(count)[None, :]).astype(np.int32)
    cols = np.arange(nlon, dtype=np.int32)
    phase = (orders[:, :, None] * cols % nlon).astype(np.float32) * np.float32(2.0 * math.pi / nlon)
    factor = np.float32(1.0 / math.sqrt(nlon))
    rows = np.stack([np.cos(phase) * factor, -np.sin(phase) * factor], axis=1)
    return rows.astype(np.float32).astype(ml_dtypes.bfloat16).reshape(slabs, 2 * count, nlon)


def reorder_matrices(rows, chans):
    out = np.zeros((2, chans, rows, rows, chans), np.float32)
    for c in range(chans):
        for k in range(rows):
            out[0, c, k, k, c] = 1
            out[1, c, k, rows - 1 - k, c] = 1
    return out.reshape(2, chans * rows, rows * chans).astype(ml_dtypes.bfloat16)


def split_orders(slab):
    if slab % 8:
        return [(0, slab)]
    units = slab // 8
    parts = min(4, units)
    sizes = [(units * (p + 1) // parts - units * p // parts) * 8 for p in range(parts)]
    starts = np.cumsum([0] + sizes)
    return [(int(s), int(n)) for s, n in zip(starts, sizes)]


def xor_pairs(size, step):
    return [(i, i ^ step) for i in range(size)]


def reorder_kernel(south_ref, pick_ref, fields_ref, out_ref):
    out_ref[0] = jnp.dot(pick_ref[0], fields_ref[0], preferred_element_type=jnp.float32).astype(out_ref.dtype)


def reorder(fields, south):
    batch, rows, chans, nlon = fields.shape
    flat = rows * chans
    picks = jnp.asarray(reorder_matrices(rows, chans))
    out = pl.pallas_call(
        reorder_kernel,
        grid_spec=pltpu.PrefetchScalarGridSpec(
            num_scalar_prefetch=1,
            grid=(batch,),
            in_specs=[
                pl.BlockSpec((1, flat, flat), lambda b, south: (south[0], 0, 0)),
                pl.BlockSpec((1, flat, nlon), lambda b, south: (b, 0, 0)),
            ],
            out_specs=pl.BlockSpec((1, flat, nlon), lambda b, south: (b, 0, 0)),
        ),
        out_shape=jax.ShapeDtypeStruct((batch, flat, nlon), fields.dtype),
        compiler_params=pltpu.CompilerParams(vmem_limit_bytes=VMEM_LIMIT),
        name="reorder",
    )(south, picks, fields.reshape(batch, flat, nlon))
    return out.reshape(batch * flat, nlon)


def dft_kernel(slabs, me_ref, rows_ref, fields_ref, *refs):
    outs, lhs = refs[:slabs], refs[slabs]
    me = me_ref[0]
    count, nlon = rows_ref.shape[1:]
    width = fields_ref.shape[0]
    joined = count % 16 == 0
    for d in range(slabs):
        lhs[d] = rows_ref[me ^ d]
    for n0 in range(0, width, 256):
        cols = slice(n0, min(n0 + 256, width))
        block = fields_ref[cols, :]
        if joined:
            res = lax.dot_general(
                lhs[...].reshape(slabs * count, nlon), block, NT, preferred_element_type=jnp.float32
            )
            for d in range(slabs):
                outs[d][:, cols] = res[d * count : (d + 1) * count].astype(jnp.bfloat16)
        else:
            for d in range(slabs):
                res = lax.dot_general(lhs[d], block, NT, preferred_element_type=jnp.float32)
                outs[d][:, cols] = res.astype(jnp.bfloat16)


def dft(flat, rows, me):
    slabs, count, nlon = rows.shape
    width = flat.shape[0]
    vmem = pl.BlockSpec(memory_space=pltpu.VMEM)
    return pl.pallas_call(
        functools.partial(dft_kernel, slabs),
        in_specs=[pl.BlockSpec(memory_space=pltpu.SMEM), vmem, vmem],
        out_specs=[vmem] * slabs,
        out_shape=[jax.ShapeDtypeStruct((count, width), jnp.bfloat16)] * slabs,
        scratch_shapes=[pltpu.VMEM((slabs, count, nlon), jnp.bfloat16)],
        compiler_params=pltpu.CompilerParams(vmem_limit_bytes=VMEM_LIMIT),
        cost_estimate=pl.CostEstimate(
            flops=2 * slabs * count * nlon * width,
            bytes_accessed=2 * (slabs * count * (nlon + width) + width * nlon),
            transcendentals=0,
        ),
        name="dft",
    )(me, jnp.asarray(rows), flat)


def packs(names, depth):
    return names % 64 == 0 and depth % LANES == 96


def packed_rows(names, depth):
    tiles = -(-depth // LANES)
    return names * depth // LANES if packs(names, depth) else names * tiles


def parity_kernel(slabs, batch, chans, band, me_ref, *refs):
    xs, out_ref, held = refs[:slabs], refs[slabs], refs[slabs + 1]
    turned = refs[slabs + 2 :]
    me = me_ref[0]
    count = xs[0].shape[0] // 2
    names = 4 * batch * chans
    depth = band * slabs // 2
    for d in range(slabs):
        held[me ^ d] = xs[d][...].astype(jnp.float32)
    for i in range(slabs // 2):
        north, south = held[i], held[slabs - 1 - i]
        held[i] = north + south
        held[slabs - 1 - i] = north - south
    for r in range(2):
        orders = slice(r * count, (r + 1) * count)
        for bc in range(batch * chans):
            lanes = slice(bc * band, (bc + 1) * band)
            for s in range(2):
                bands = [i if s == 0 else slabs - 1 - i for i in range(slabs // 2)]
                line = jnp.concatenate([held[i, orders, lanes] for i in bands], axis=1)
                name = (s * batch * chans + bc) * 2 + r
                for t, tile in enumerate(turned):
                    piece = line[:, t * LANES : min((t + 1) * LANES, depth)]
                    if piece.shape[1] < LANES:
                        blank = jnp.zeros((count, LANES - piece.shape[1]), jnp.float32)
                        piece = jnp.concatenate([piece, blank], axis=1)
                    tile[pl.ds(name, count, stride=names), :] = piece
    packed = packs(names, depth)

    def write(m, carry):
        rows = pl.ds(pl.multiple_of(m * names, names), names)
        for t, tile in enumerate(turned):
            block = tile[rows, :].astype(jnp.bfloat16)
            if packed and t == len(turned) - 1:
                step = names // 4
                last = block[3 * step :]
                for g in range(3):
                    both = jnp.concatenate(
                        [block[g * step : (g + 1) * step, :96], last[:, 32 * g : 32 * (g + 1)]], axis=1
                    )
                    out_ref[m, t * names + g * step : t * names + (g + 1) * step, :] = both
            else:
                out_ref[m, t * names : (t + 1) * names, :] = block
        return carry

    lax.fori_loop(0, count, write, 0)


def parity(blocks, me, batch, chans, band):
    slabs = len(blocks)
    count = blocks[0].shape[0] // 2
    width = blocks[0].shape[1]
    names = 4 * batch * chans
    depth = band * slabs // 2
    vmem = pl.BlockSpec(memory_space=pltpu.VMEM)
    total = packed_rows(names, depth)
    return pl.pallas_call(
        functools.partial(parity_kernel, slabs, batch, chans, band),
        in_specs=[pl.BlockSpec(memory_space=pltpu.SMEM)] + [vmem] * slabs,
        out_specs=vmem,
        out_shape=jax.ShapeDtypeStruct((count, total, LANES), jnp.bfloat16),
        scratch_shapes=[pltpu.VMEM((slabs, 2 * count, width), jnp.float32)]
        + [pltpu.VMEM((count * names, LANES), jnp.float32)] * -(-depth // LANES),
        compiler_params=pltpu.CompilerParams(vmem_limit_bytes=VMEM_LIMIT),
        cost_estimate=pl.CostEstimate(
            flops=40 * slabs * count * width, bytes_accessed=8 * slabs * count * width, transcendentals=0
        ),
        name="parity",
    )(me, *blocks)


def project_kernel(groups, batch, first, info_ref, table_ref, *refs):
    parts, out_ref, rhs = refs[:groups], refs[-2], refs[-1]
    me, odd = info_ref[0], info_ref[1]
    orders, degrees, depth = table_ref.shape
    inner = rhs.shape[3]
    names = 2 * batch * inner
    packed = packs(names, depth)
    tiles = -(-depth // LANES)
    for m in range(orders):
        for d in range(groups):
            ch = me ^ d
            for sb in range(2 * batch):
                for t in range(tiles):
                    width = min(LANES, depth - t * LANES)
                    base = t * names
                    if packed and t == tiles - 1:
                        step = names // 4
                        if (sb + 1) * inner <= 3 * step:
                            block = parts[d][m, base + sb * inner : base + (sb + 1) * inner, :width]
                        else:
                            off = sb * inner - 3 * step
                            block = jnp.concatenate(
                                [
                                    parts[d][m, base + g * step + off : base + g * step + off + inner, 96:]
                                    for g in range(3)
                                ],
                                axis=1,
                            )
                    else:
                        block = parts[d][m, base + sb * inner : base + (sb + 1) * inner, :width]
                    rhs[m, sb, ch, :, t * LANES : t * LANES + width] = block
    row = lax.broadcasted_iota(jnp.int32, (degrees, batch * groups * inner), 0)
    start = pl.program_id(0) * orders + first
    for m in range(orders):
        right = rhs[m].reshape(2 * batch * groups * inner, depth)
        both = lax.dot_general(table_ref[m], right, NT, preferred_element_type=jnp.float32)
        cut = batch * groups * inner
        even = ((row + (odd + start + m)) & 1) == 0
        out_ref[m] = jnp.where(even, both[:, :cut], both[:, cut:])


def project(table, parts, info, first, batch, inner, prior):
    slab, degrees, depth = table.shape
    groups = len(parts)
    count, total, _ = parts[0].shape
    step = 8 if count % 8 == 0 else count
    lead = first // step
    names = batch * groups * inner
    operands = [info, table, *parts]
    in_specs = [
        pl.BlockSpec(memory_space=pltpu.SMEM),
        pl.BlockSpec((step, degrees, depth), lambda g: (g + lead, 0, 0)),
    ] + [pl.BlockSpec((step, total, LANES), lambda g: (g, 0, 0))] * groups
    aliases = {}
    if prior is not None:
        operands.append(prior)
        in_specs.append(pl.BlockSpec(memory_space=pl.ANY))
        aliases = {len(operands) - 1: 0}
    return pl.pallas_call(
        functools.partial(project_kernel, groups, batch, first),
        grid=(count // step,),
        in_specs=in_specs,
        out_specs=pl.BlockSpec((step, degrees, names), lambda g: (g + lead, 0, 0)),
        out_shape=jax.ShapeDtypeStruct((slab, degrees, names), jnp.float32),
        scratch_shapes=[pltpu.VMEM((step, 2 * batch, groups, inner, depth), jnp.bfloat16)],
        input_output_aliases=aliases,
        compiler_params=pltpu.CompilerParams(vmem_limit_bytes=VMEM_LIMIT),
        cost_estimate=pl.CostEstimate(
            flops=4 * count * degrees * depth * names,
            bytes_accessed=count * degrees * (2 * depth + 4 * names) + 2 * groups * count * total * LANES,
            transcendentals=0,
        ),
        name="project",
    )(*operands)


def shards(slabs, groups, fields, table):
    batch, band, chans, nlon = fields.shape
    slab, degrees, depth = table.shape
    lat, ch = lax.axis_index("lat"), lax.axis_index("ch")
    me = lat.astype(jnp.int32).reshape(1)
    south = (me >= slabs // 2).astype(jnp.int32)
    odd = (ch * degrees + lat * slab) % 2
    info = jnp.stack([ch, odd]).astype(jnp.int32)
    flat = reorder(fields, south)
    chunks = split_orders(slab)
    out = None
    for q, (first, count) in enumerate(chunks):
        sends = dft(flat, fourier_rows(nlon, slabs, slab, (first, count)), me)
        blocks = [sends[0]] + [
            lax.ppermute(sends[d], "lat", xor_pairs(slabs, d)) for d in range(1, slabs)
        ]
        mine = parity(blocks, me, batch, chans, band)
        bits = [1 << k for k in range(groups.bit_length() - 1)]
        if q % 2:
            bits = bits[::-1]
        parts = {0: mine}
        for bit in bits:
            parts.update({d ^ bit: lax.ppermute(parts[d], "ch", xor_pairs(groups, bit)) for d in list(parts)})
        out = project(table, [parts[d] for d in range(groups)], info, first, batch, 2 * chans, out)
    return out


def solution(mesh):
    return jax.shard_map(
        functools.partial(shards, mesh.shape["lat"], mesh.shape["ch"]),
        mesh=mesh,
        in_specs=(P(None, "lat", "ch", None), P("lat", "ch", None)),
        out_specs=P("lat", "ch", None),
        check_vma=False,
    )
```

```python
import functools
import math

import jax
import jax.numpy as jnp
import ml_dtypes
import numpy as np
from jax import lax
from jax.experimental import pallas as pl
from jax.experimental.pallas import tpu as pltpu
from jax.sharding import PartitionSpec as P

LANES = 128
VMEM_LIMIT = 32 * 1024 * 1024
SMALL = pl.CostEstimate(flops=1, bytes_accessed=1, transcendentals=0)
NT = (((1,), (1,)), ((), ()))


def fourier_rows(nlon, slabs, slab, chunk):
    first, count = chunk
    orders = (np.arange(slabs)[:, None] * slab + first + np.arange(count)[None, :]).astype(np.int32)
    cols = np.arange(nlon, dtype=np.int32)
    phase = (orders[:, :, None] * cols % nlon).astype(np.float32) * np.float32(2.0 * math.pi / nlon)
    factor = np.float32(1.0 / math.sqrt(nlon))
    rows = np.stack([np.cos(phase) * factor, -np.sin(phase) * factor], axis=1)
    rows = rows.astype(np.float32).astype(ml_dtypes.bfloat16).reshape(slabs // 2, 2, 2 * count, nlon)
    return np.pad(rows.transpose(1, 0, 2, 3), [(0, 0)] * 3 + [(0, -nlon % LANES)])


def reorder_groups(rows, chans):
    step = max(8, 256 // chans // 8 * 8)
    return [(k, min(step, rows - k)) for k in range(0, rows, step)]


def reorder_matrices(count, chans):
    out = np.zeros((2, chans, count, count, chans), np.float32)
    for c in range(chans):
        for k in range(count):
            out[0, c, k, k, c] = 1
            out[1, c, k, count - 1 - k, c] = 1
    return out.reshape(2, chans * count, count * chans).astype(ml_dtypes.bfloat16)


def split_orders(slab):
    if slab % 8:
        return [(0, slab)]
    units = slab // 8
    parts = min(4, units)
    sizes = [(units * (p + 1) // parts - units * p // parts) * 8 for p in range(parts)]
    starts = np.cumsum([0] + sizes)
    return [(int(s), int(n)) for s, n in zip(starts, sizes)]


def xor_pairs(size, step):
    return [(i, i ^ step) for i in range(size)]


def reorder_kernel(rows, chans, south_ref, fields_ref, *refs):
    picks, out_ref = refs[:-1], refs[-1]
    south = south_ref[0]
    for (k, count), pick in zip(reorder_groups(rows, chans), picks):
        start = jnp.where(south == 1, rows - k - count, k) * chans
        block = fields_ref[0, pl.ds(pl.multiple_of(start, 8 * chans), count * chans), :]
        res = jnp.dot(pick[0], block, preferred_element_type=jnp.float32).astype(out_ref.dtype)
        for c in range(chans):
            out_ref[0, c * rows + k : c * rows + k + count, : res.shape[1]] = res[c * count : (c + 1) * count]
    blank = out_ref.shape[2] - fields_ref.shape[2]
    if blank:
        out_ref[0, :, fields_ref.shape[2] :] = jnp.zeros((rows * chans, blank), out_ref.dtype)


def reorder(fields, south):
    batch, rows, chans, nlon = fields.shape
    flat, padded = rows * chans, -(-nlon // LANES) * LANES
    picks = [jnp.asarray(reorder_matrices(count, chans)) for _, count in reorder_groups(rows, chans)]
    out = pl.pallas_call(
        functools.partial(reorder_kernel, rows, chans),
        grid_spec=pltpu.PrefetchScalarGridSpec(
            num_scalar_prefetch=1,
            grid=(batch,),
            in_specs=[pl.BlockSpec((1, flat, nlon), lambda b, south: (b, 0, 0))]
            + [pl.BlockSpec((1,) + p.shape[1:], lambda b, south: (south[0], 0, 0)) for p in picks],
            out_specs=pl.BlockSpec((1, flat, padded), lambda b, south: (b, 0, 0)),
        ),
        out_shape=jax.ShapeDtypeStruct((batch, flat, padded), fields.dtype),
        compiler_params=pltpu.CompilerParams(vmem_limit_bytes=VMEM_LIMIT),
        cost_estimate=SMALL,
        name="reorder",
    )(south, fields.reshape(batch, flat, nlon), *picks)
    return out.reshape(batch * flat, padded)


def dft_kernel(chips, bands, where_ref, rows_ref, *refs):
    fields, outs, lhs = refs[:bands], refs[-1 - chips : -1], refs[-1]
    chip = where_ref[1]
    count, nlon = rows_ref.shape[2:]
    width = fields[0].shape[0]
    joined = count % 16 == 0
    for d in range(chips):
        lhs[d] = rows_ref[0, chip ^ d]
    for j in range(bands):
        for n0 in range(0, width, 256):
            cols = slice(n0, min(n0 + 256, width))
            block = fields[j][cols, :]
            if joined:
                res = lax.dot_general(
                    lhs[...].reshape(chips * count, nlon), block, NT, preferred_element_type=jnp.float32
                )
                for d in range(chips):
                    outs[d][j, :, cols] = res[d * count : (d + 1) * count].astype(jnp.bfloat16)
            else:
                for d in range(chips):
                    res = lax.dot_general(lhs[d], block, NT, preferred_element_type=jnp.float32)
                    outs[d][j, :, cols] = res.astype(jnp.bfloat16)


def dft(flats, rows, where, after=None):
    _, chips, count, nlon = rows.shape
    width = flats[0].shape[0]
    bands = len(flats)
    whole = pl.BlockSpec((width, nlon), lambda g, where: (0, 0))
    operands = [where, jnp.asarray(rows), *flats]
    in_specs = [pl.BlockSpec((1, chips, count, nlon), lambda g, where: (where[0], 0, 0, 0))] + [whole] * bands
    if after is not None:
        operands.append(after)
        in_specs.append(pl.BlockSpec(memory_space=pl.ANY))
    return pl.pallas_call(
        functools.partial(dft_kernel, chips, bands),
        grid_spec=pltpu.PrefetchScalarGridSpec(
            num_scalar_prefetch=1,
            grid=(1,),
            in_specs=in_specs,
            out_specs=[pl.BlockSpec((bands, count, width), lambda g, where: (0, 0, 0))] * chips,
            scratch_shapes=[pltpu.VMEM((chips, count, nlon), jnp.bfloat16)],
        ),
        out_shape=[jax.ShapeDtypeStruct((bands, count, width), jnp.bfloat16)] * chips,
        compiler_params=pltpu.CompilerParams(vmem_limit_bytes=VMEM_LIMIT),
        cost_estimate=SMALL,
        name="dft",
    )(*operands)


def gate(arrays, after):
    anywhere = pl.BlockSpec(memory_space=pl.ANY)
    return pl.pallas_call(
        lambda *refs: None,
        in_specs=[anywhere] * (len(arrays) + len(after)),
        out_specs=[anywhere] * len(arrays),
        out_shape=[jax.ShapeDtypeStruct(a.shape, a.dtype) for a in arrays],
        input_output_aliases={i: i for i in range(len(arrays))},
        cost_estimate=SMALL,
        name="gate",
    )(*arrays, *after)


def packs(names, depth):
    return names % 64 == 0 and depth % LANES == 96


def packed_rows(names, depth):
    tiles = -(-depth // LANES)
    return names * depth // LANES if packs(names, depth) else names * tiles


def parity_kernel(slabs, sources, batch, chans, band, me_ref, *refs):
    xs, (_, out_ref, held, *turned) = refs[: len(sources)], refs[len(sources) :]
    me = me_ref[0]
    count = xs[0].shape[1] // 2
    names = 4 * batch * chans
    depth = band * slabs // 2
    for x, steps in zip(xs, sources):
        for j, d in enumerate(steps):
            held[me ^ d] = x[j].astype(jnp.float32)
    for i in range(slabs // 2):
        north, south = held[i], held[slabs - 1 - i]
        held[i] = north + south
        held[slabs - 1 - i] = north - south
    for r in range(2):
        orders = slice(r * count, (r + 1) * count)
        for bc in range(batch * chans):
            lanes = slice(bc * band, (bc + 1) * band)
            for s in range(2):
                bands = [i if s == 0 else slabs - 1 - i for i in range(slabs // 2)]
                line = jnp.concatenate([held[i, orders, lanes] for i in bands], axis=1)
                name = (s * batch * chans + bc) * 2 + r
                for t, tile in enumerate(turned):
                    piece = line[:, t * LANES : min((t + 1) * LANES, depth)]
                    if piece.shape[1] < LANES:
                        blank = jnp.zeros((count, LANES - piece.shape[1]), jnp.float32)
                        piece = jnp.concatenate([piece, blank], axis=1)
                    tile[pl.ds(name, count, stride=names), :] = piece
    packed = packs(names, depth)

    def write(m, carry):
        rows = pl.ds(pl.multiple_of(m * names, names), names)
        for t, tile in enumerate(turned):
            block = tile[rows, :].astype(jnp.bfloat16)
            if packed and t == len(turned) - 1:
                step = names // 4
                last = block[3 * step :]
                for g in range(3):
                    both = jnp.concatenate(
                        [block[g * step : (g + 1) * step, :96], last[:, 32 * g : 32 * (g + 1)]], axis=1
                    )
                    out_ref[m, t * names + g * step : t * names + (g + 1) * step, :] = both
            else:
                out_ref[m, t * names : (t + 1) * names, :] = block
        return carry

    lax.fori_loop(0, count, write, 0)


def parity(blocks, sources, me, slabs, batch, chans, band, after):
    count = blocks[0].shape[1] // 2
    width = blocks[0].shape[2]
    names = 4 * batch * chans
    depth = band * slabs // 2
    vmem = pl.BlockSpec(memory_space=pltpu.VMEM)
    total = packed_rows(names, depth)
    return pl.pallas_call(
        functools.partial(parity_kernel, slabs, sources, batch, chans, band),
        in_specs=[pl.BlockSpec(memory_space=pltpu.SMEM)] + [vmem] * len(blocks) + [pl.BlockSpec(memory_space=pl.ANY)],
        out_specs=vmem,
        out_shape=jax.ShapeDtypeStruct((count, total, LANES), jnp.bfloat16),
        scratch_shapes=[pltpu.VMEM((slabs, 2 * count, width), jnp.float32)]
        + [pltpu.VMEM((count * names, LANES), jnp.float32)] * -(-depth // LANES),
        compiler_params=pltpu.CompilerParams(vmem_limit_bytes=VMEM_LIMIT),
        cost_estimate=SMALL,
        name="parity",
    )(me, *blocks, after)


def project_kernel(groups, batch, first, info_ref, table_ref, *refs):
    parts, out_ref, rhs = refs[:groups], refs[-2], refs[-1]
    me, odd = info_ref[0], info_ref[1]
    orders, degrees, depth = table_ref.shape
    inner = rhs.shape[3]
    names = 2 * batch * inner
    packed = packs(names, depth)
    tiles = -(-depth // LANES)
    for m in range(orders):
        for d in range(groups):
            ch = me ^ d
            for sb in range(2 * batch):
                for t in range(tiles):
                    width = min(LANES, depth - t * LANES)
                    base = t * names
                    if packed and t == tiles - 1:
                        step = names // 4
                        if (sb + 1) * inner <= 3 * step:
                            block = parts[d][m, base + sb * inner : base + (sb + 1) * inner, :width]
                        else:
                            off = sb * inner - 3 * step
                            block = jnp.concatenate(
                                [
                                    parts[d][m, base + g * step + off : base + g * step + off + inner, 96:]
                                    for g in range(3)
                                ],
                                axis=1,
                            )
                    else:
                        block = parts[d][m, base + sb * inner : base + (sb + 1) * inner, :width]
                    rhs[m, sb, ch, :, t * LANES : t * LANES + width] = block
    row = lax.broadcasted_iota(jnp.int32, (degrees, batch * groups * inner), 0)
    start = pl.program_id(0) * orders + first
    for m in range(orders):
        right = rhs[m].reshape(2 * batch * groups * inner, depth)
        both = lax.dot_general(table_ref[m], right, NT, preferred_element_type=jnp.float32)
        cut = batch * groups * inner
        even = ((row + (odd + start + m)) & 1) == 0
        out_ref[m] = jnp.where(even, both[:, :cut], both[:, cut:])


def project(table, parts, starts, count, info, first, batch, inner, prior, after):
    slab, degrees, depth = table.shape
    groups = len(parts)
    total = parts[0].shape[1]
    step = 4 if count % 4 == 0 and first % 4 == 0 else count
    lead = first // step
    names = batch * groups * inner
    operands = [info, table, *parts]
    in_specs = [
        pl.BlockSpec(memory_space=pltpu.SMEM),
        pl.BlockSpec((step, degrees, depth), lambda g: (g + lead, 0, 0)),
    ] + [
        pl.BlockSpec((step, total, LANES), functools.partial(lambda skip, g: (g + skip, 0, 0), start // step))
        for start in starts
    ]
    aliases = {}
    if after is not None:
        operands.append(after)
        in_specs.append(pl.BlockSpec(memory_space=pl.ANY))
    if prior is not None:
        operands.append(prior)
        in_specs.append(pl.BlockSpec(memory_space=pl.ANY))
        aliases = {len(operands) - 1: 0}
    return pl.pallas_call(
        functools.partial(project_kernel, groups, batch, first),
        grid=(count // step,),
        in_specs=in_specs,
        out_specs=pl.BlockSpec((step, degrees, names), lambda g: (g + lead, 0, 0)),
        out_shape=jax.ShapeDtypeStruct((slab, degrees, names), jnp.float32),
        scratch_shapes=[pltpu.VMEM((step, 2 * batch, groups, inner, depth), jnp.bfloat16)],
        input_output_aliases=aliases,
        compiler_params=pltpu.CompilerParams(vmem_limit_bytes=VMEM_LIMIT),
        cost_estimate=SMALL,
        name="project",
    )(*operands)


def shards(slabs, groups, fields, table):
    batch, band, chans, nlon = fields.shape
    slab, degrees, depth = table.shape
    chips = slabs // 2
    lat, ch = lax.axis_index("lat").astype(jnp.int32), lax.axis_index("ch").astype(jnp.int32)
    me = lat.reshape(1)
    where = jnp.stack([lat % 2, lat // 2])
    south = (me >= chips).astype(jnp.int32)
    info = jnp.stack([ch, (ch * degrees + lat * slab) % 2])
    chunks = split_orders(slab)
    tables = [fourier_rows(nlon, slabs, slab, chunk) for chunk in chunks]

    own = reorder(fields, south)
    other = lax.ppermute(own, "lat", xor_pairs(slabs, 1))

    def send(block, d):
        return lax.ppermute(block, "lat", xor_pairs(slabs, 2 * d))

    def pass_on(block, bit):
        return lax.ppermute(block, "ch", xor_pairs(groups, bit))

    near = dft([own], tables[0], where)
    far = dft([other], tables[0], where, near[0])
    blocks = [near[0]] + [send(near[d], d) for d in range(1, chips)]
    arrived = [far[0]] + [send(far[d], d) for d in range(1, chips)]
    blocks = blocks + arrived
    sources = tuple((2 * d,) for d in range(chips)) + tuple((2 * d + 1,) for d in range(chips))

    bits = [1 << k for k in range(groups.bit_length() - 1)]
    last, total = far[0], len(chunks)
    waiting, out = [], None

    def forwarded(parts, q, after):
        first, second = (bits[0], bits[1]) if q % 2 == 0 else (bits[1], bits[0])
        count = parts[0].shape[0]
        if q < total - 1 or count % 8:
            held = gate([parts[first]], [parts[second], after])
            parts[first] = held[0]
            return [(0, count, pass_on(held[0], second))], held[0]
        half = count // 2
        held = gate([parts[first][:half], parts[second][half:]], [after])
        return [(0, half, pass_on(held[0], second)), (half, half, pass_on(held[1], first))], held[0]

    def finish(item, prior, after):
        first, parts, pieces = item
        for start, count, piece in pieces:
            arrays = [parts[d] for d in range(groups - 1)] + [piece]
            starts = [start] * (groups - 1) + [0]
            prior = project(table, arrays, starts, count, info, first + start, batch, 2 * chans, prior, after)
        return prior

    if groups != 4 or chips < 3:
        for q, (first, count) in enumerate(chunks):
            if q:
                sends = dft([own, other], tables[q], where, last)
                blocks = [sends[0]] + [send(sends[d], d) for d in range(1, chips)]
                sources = tuple((2 * d, 2 * d + 1) for d in range(chips))
            last = parity(blocks, sources, me, slabs, batch, chans, band, last)
            parts = [last]
            for bit in bits:
                parts += [pass_on(part, bit) for part in parts]
            out = project(table, parts, [0] * groups, count, info, first, batch, 2 * chans, out, last)
        return out

    ready = []
    for q in range(total):
        more = q + 1 < total
        if more:
            sends = dft([own, other], tables[q + 1], where, last)
            early = gate(sends[1:-1], arrived[1:])
            last = early[0]
        if q == 1:
            pieces, last = forwarded(waiting[0], 0, last)
            ready.append((chunks[0][0], waiting.pop(0), pieces))
        if q >= 2 and more:
            out = finish(ready.pop(0), out, last)
            last = out
        mine = parity(blocks, sources, me, slabs, batch, chans, band, last)
        last = mine
        parts = {0: mine}
        for bit in bits:
            parts[bit] = pass_on(mine, bit)
        if q >= 2:
            pieces, last = forwarded(waiting[0], q - 1, last)
            ready.append((chunks[q - 1][0], waiting.pop(0), pieces))
        waiting.append(parts)
        if more:
            arrived = [sends[0]] + [send(early[d - 1], d) for d in range(1, chips - 1)]
            late = gate(sends[-1:], [arrived[1], last])
            last = late[0]
            arrived.append(send(late[0], chips - 1))
            blocks = arrived
            sources = tuple((2 * d, 2 * d + 1) for d in range(chips))
    while len(ready) > 1:
        out = finish(ready.pop(0), out, last)
        last = out
    pieces, last = forwarded(waiting[0], total - 1, last)
    ready.append((chunks[-1][0], waiting.pop(0), pieces))
    while ready:
        out = finish(ready.pop(0), out, last)
        last = out
    return out


def solution(mesh):
    return jax.shard_map(
        functools.partial(shards, mesh.shape["lat"], mesh.shape["ch"]),
        mesh=mesh,
        in_specs=(P(None, "lat", "ch", None), P("lat", "ch", None)),
        out_specs=P("lat", "ch", None),
        check_vma=False,
    )
```

```python
import functools
import math

import jax
import jax.numpy as jnp
import ml_dtypes
import numpy as np
from jax import lax
from jax.experimental import pallas as pl
from jax.experimental.pallas import tpu as pltpu
from jax.sharding import PartitionSpec as P

LANES = 128
SHARES = (2 / 11, 4 / 11, 7 / 11, 1)
VMEM_LIMIT = 60 * 1024 * 1024
SMALL = pl.CostEstimate(flops=1, bytes_accessed=1, transcendentals=0)
NT = (((1,), (1,)), ((), ()))


def fourier_rows(nlon, slabs, slab, chunk):
    first, count = chunk
    orders = (np.arange(slabs)[:, None] * slab + first + np.arange(count)[None, :]).astype(np.int32)
    cols = np.arange(nlon, dtype=np.int32)
    phase = (orders[:, :, None] * cols % nlon).astype(np.float32) * np.float32(2.0 * math.pi / nlon)
    factor = np.float32(1.0 / math.sqrt(nlon))
    rows = np.stack([np.cos(phase) * factor, -np.sin(phase) * factor], axis=1)
    rows = rows.astype(np.float32).astype(ml_dtypes.bfloat16).reshape(slabs // 2, 2, 2 * count, nlon)
    return np.pad(rows.transpose(1, 0, 2, 3), [(0, 0)] * 3 + [(0, -nlon % LANES)])


def reorder_groups(rows, chans):
    step = max(8, 256 // chans // 8 * 8)
    return [(k, min(step, rows - k)) for k in range(0, rows, step)]


def reorder_matrices(count, chans):
    out = np.zeros((2, chans, count, count, chans), np.float32)
    for c in range(chans):
        for k in range(count):
            out[0, c, k, k, c] = 1
            out[1, c, k, count - 1 - k, c] = 1
    return out.reshape(2, chans * count, count * chans).astype(ml_dtypes.bfloat16)


def split_orders(slab):
    if slab % 8:
        return [(0, slab)]
    units = slab // 8
    ends = [round(units * share) for share in SHARES]
    return [(8 * lo, 8 * (hi - lo)) for lo, hi in zip([0] + ends, ends) if hi > lo]


def xor_pairs(size, step):
    return [(i, i ^ step) for i in range(size)]


def reorder_kernel(rows, chans, south_ref, fields_ref, *refs):
    picks, out_ref = refs[:-1], refs[-1]
    south = south_ref[0]
    for (k, count), pick in zip(reorder_groups(rows, chans), picks):
        start = jnp.where(south == 1, rows - k - count, k) * chans
        block = fields_ref[0, pl.ds(pl.multiple_of(start, 8 * chans), count * chans), :]
        res = jnp.dot(pick[0], block, preferred_element_type=jnp.float32).astype(out_ref.dtype)
        for c in range(chans):
            out_ref[0, c * rows + k : c * rows + k + count, : res.shape[1]] = res[c * count : (c + 1) * count]
    blank = out_ref.shape[2] - fields_ref.shape[2]
    if blank:
        out_ref[0, :, fields_ref.shape[2] :] = jnp.zeros((rows * chans, blank), out_ref.dtype)


def reorder(fields, south):
    batch, rows, chans, nlon = fields.shape
    flat, padded = rows * chans, -(-nlon // LANES) * LANES
    picks = [jnp.asarray(reorder_matrices(count, chans)) for _, count in reorder_groups(rows, chans)]
    out = pl.pallas_call(
        functools.partial(reorder_kernel, rows, chans),
        grid_spec=pltpu.PrefetchScalarGridSpec(
            num_scalar_prefetch=1,
            grid=(batch,),
            in_specs=[pl.BlockSpec((1, flat, nlon), lambda b, south: (b, 0, 0))]
            + [pl.BlockSpec((1,) + p.shape[1:], lambda b, south: (south[0], 0, 0)) for p in picks],
            out_specs=pl.BlockSpec((1, flat, padded), lambda b, south: (b, 0, 0)),
        ),
        out_shape=jax.ShapeDtypeStruct((batch, flat, padded), fields.dtype),
        compiler_params=pltpu.CompilerParams(vmem_limit_bytes=VMEM_LIMIT),
        cost_estimate=SMALL,
        name="reorder",
    )(south, fields.reshape(batch, flat, nlon), *picks)
    return out.reshape(batch * flat, padded)


def dft_kernel(chips, counts, layout, bands, where_ref, rows_ref, *refs):
    fields, outs, lhs = refs[:bands], refs[-1 - len(layout) : -1], refs[-1]
    chip = where_ref[1]
    total = sum(counts)
    width = fields[0].shape[0]
    firsts = np.cumsum([0] + list(counts))
    aligned = all(n % 16 == 0 for n in counts)
    for d in range(chips):
        if aligned:
            lhs[d * total : (d + 1) * total] = rows_ref[0, chip ^ d]
    for j in range(bands):
        for n0 in range(0, width, 256):
            cols = slice(n0, min(n0 + 256, width))
            block = fields[j][cols, :]
            if aligned:
                res = lax.dot_general(lhs[...], block, NT, preferred_element_type=jnp.float32)
            for out, (d, lo, hi) in zip(outs, layout):
                if aligned:
                    part = res[d * total + firsts[lo] : d * total + firsts[hi]]
                else:
                    part = lax.dot_general(rows_ref[0, chip ^ d], block, NT, preferred_element_type=jnp.float32)
                out[j, :, cols] = part.astype(jnp.bfloat16)


def dft(flats, rows, counts, layout, where, after, band=0, whole=0, prior=()):
    _, chips, total, nlon = rows.shape
    width = flats[0].shape[0]
    bands = len(flats)
    operands = [where, jnp.asarray(rows), *flats, after, *prior]
    anywhere = pl.BlockSpec(memory_space=pl.ANY)
    sizes = [sum(counts[lo:hi]) for _, lo, hi in layout]
    return pl.pallas_call(
        functools.partial(dft_kernel, chips, counts, layout, bands),
        grid_spec=pltpu.PrefetchScalarGridSpec(
            num_scalar_prefetch=1,
            grid=(1,),
            in_specs=[pl.BlockSpec((1, chips, total, nlon), lambda g, where: (where[0], 0, 0, 0))]
            + [pl.BlockSpec((width, nlon), lambda g, where: (0, 0))] * bands
            + [anywhere] * (1 + len(prior)),
            out_specs=[pl.BlockSpec((bands, n, width), lambda g, where: (band, 0, 0)) for n in sizes],
            scratch_shapes=[pltpu.VMEM((chips * total, nlon), jnp.bfloat16)],
        ),
        out_shape=[jax.ShapeDtypeStruct((whole or bands, n, width), jnp.bfloat16) for n in sizes],
        input_output_aliases={3 + bands + i: i for i in range(len(prior))},
        compiler_params=pltpu.CompilerParams(vmem_limit_bytes=VMEM_LIMIT),
        cost_estimate=SMALL,
        name="dft",
    )(*operands)


def gate(arrays, after):
    anywhere = pl.BlockSpec(memory_space=pl.ANY)
    return pl.pallas_call(
        lambda *refs: None,
        in_specs=[anywhere] * (len(arrays) + len(after)),
        out_specs=[anywhere] * len(arrays),
        out_shape=[jax.ShapeDtypeStruct(a.shape, a.dtype) for a in arrays],
        input_output_aliases={i: i for i in range(len(arrays))},
        cost_estimate=SMALL,
        name="gate",
    )(*arrays, *after)


def packs(names, depth):
    return names % 64 == 0 and depth % LANES == 96


def packed_rows(names, depth):
    tiles = -(-depth // LANES)
    return names * depth // LANES if packs(names, depth) else names * tiles


def parity_kernel(slabs, sources, count, batch, chans, band, me_ref, *refs):
    xs, (_, out_ref, held, *turned) = refs[: len(sources)], refs[len(sources) :]
    me = me_ref[0]
    names = 4 * batch * chans
    depth = band * slabs // 2
    for x, (chip, start) in zip(xs, sources):
        for j in range(2):
            held[me ^ (2 * chip + j)] = x[j, start : start + 2 * count].astype(jnp.float32)
    for i in range(slabs // 2):
        north, south = held[i], held[slabs - 1 - i]
        held[i] = north + south
        held[slabs - 1 - i] = north - south
    for r in range(2):
        orders = slice(r * count, (r + 1) * count)
        for bc in range(batch * chans):
            lanes = slice(bc * band, (bc + 1) * band)
            for s in range(2):
                bands = [i if s == 0 else slabs - 1 - i for i in range(slabs // 2)]
                line = jnp.concatenate([held[i, orders, lanes] for i in bands], axis=1)
                name = (s * batch * chans + bc) * 2 + r
                for t, tile in enumerate(turned):
                    piece = line[:, t * LANES : min((t + 1) * LANES, depth)]
                    if piece.shape[1] < LANES:
                        blank = jnp.zeros((count, LANES - piece.shape[1]), jnp.float32)
                        piece = jnp.concatenate([piece, blank], axis=1)
                    tile[pl.ds(name, count, stride=names), :] = piece
    packed = packs(names, depth)

    def write(m, carry):
        rows = pl.ds(pl.multiple_of(m * names, names), names)
        for t, tile in enumerate(turned):
            block = tile[rows, :].astype(jnp.bfloat16)
            if packed and t == len(turned) - 1:
                step = names // 4
                last = block[3 * step :]
                for g in range(3):
                    both = jnp.concatenate(
                        [block[g * step : (g + 1) * step, :96], last[:, 32 * g : 32 * (g + 1)]], axis=1
                    )
                    out_ref[m, t * names + g * step : t * names + (g + 1) * step, :] = both
            else:
                out_ref[m, t * names : (t + 1) * names, :] = block
        return carry

    lax.fori_loop(0, count, write, 0)


def parity(blocks, sources, count, me, slabs, batch, chans, band, after):
    width = blocks[0].shape[2]
    names = 4 * batch * chans
    depth = band * slabs // 2
    total = packed_rows(names, depth)
    return pl.pallas_call(
        functools.partial(parity_kernel, slabs, sources, count, batch, chans, band),
        grid=(1,),
        in_specs=[pl.BlockSpec(memory_space=pltpu.SMEM)]
        + [pl.BlockSpec(block.shape, lambda g: (0, 0, 0)) for block in blocks]
        + [pl.BlockSpec(memory_space=pl.ANY)],
        out_specs=pl.BlockSpec((count, total, LANES), lambda g: (0, 0, 0)),
        out_shape=jax.ShapeDtypeStruct((count, total, LANES), jnp.bfloat16),
        scratch_shapes=[pltpu.VMEM((slabs, 2 * count, width), jnp.float32)]
        + [pltpu.VMEM((count * names, LANES), jnp.float32)] * -(-depth // LANES),
        compiler_params=pltpu.CompilerParams(vmem_limit_bytes=VMEM_LIMIT),
        cost_estimate=SMALL,
        name="parity",
    )(me, *blocks, after)


def project_kernel(groups, batch, first, info_ref, table_ref, *refs):
    parts, out_ref, rhs = refs[:groups], refs[-2], refs[-1]
    me, odd = info_ref[0], info_ref[1]
    orders, degrees, depth = table_ref.shape
    inner = rhs.shape[3]
    names = 2 * batch * inner
    packed = packs(names, depth)
    tiles = -(-depth // LANES)
    for m in range(orders):
        for d in range(groups):
            ch = me ^ d
            for sb in range(2 * batch):
                for t in range(tiles):
                    width = min(LANES, depth - t * LANES)
                    base = t * names
                    if packed and t == tiles - 1:
                        step = names // 4
                        if (sb + 1) * inner <= 3 * step:
                            block = parts[d][m, base + sb * inner : base + (sb + 1) * inner, :width]
                        else:
                            off = sb * inner - 3 * step
                            block = jnp.concatenate(
                                [
                                    parts[d][m, base + g * step + off : base + g * step + off + inner, 96:]
                                    for g in range(3)
                                ],
                                axis=1,
                            )
                    else:
                        block = parts[d][m, base + sb * inner : base + (sb + 1) * inner, :width]
                    rhs[m, sb, ch, :, t * LANES : t * LANES + width] = block
    row = lax.broadcasted_iota(jnp.int32, (degrees, batch * groups * inner), 0)
    start = pl.program_id(0) * orders + first
    for m in range(orders):
        right = rhs[m].reshape(2 * batch * groups * inner, depth)
        both = lax.dot_general(table_ref[m], right, NT, preferred_element_type=jnp.float32)
        cut = batch * groups * inner
        even = ((row + (odd + start + m)) & 1) == 0
        out_ref[m] = jnp.where(even, both[:, :cut], both[:, cut:])


def project(table, parts, starts, count, info, first, batch, inner, prior, after):
    slab, degrees, depth = table.shape
    groups = len(parts)
    total = parts[0].shape[1]
    step = 4 if count % 4 == 0 and first % 4 == 0 else count
    lead = first // step
    names = batch * groups * inner
    operands = [info, table, *parts]
    in_specs = [
        pl.BlockSpec(memory_space=pltpu.SMEM),
        pl.BlockSpec((step, degrees, depth), lambda g: (g + lead, 0, 0)),
    ] + [
        pl.BlockSpec((step, total, LANES), functools.partial(lambda skip, g: (g + skip, 0, 0), start // step))
        for start in starts
    ]
    aliases = {}
    if after is not None:
        operands.append(after)
        in_specs.append(pl.BlockSpec(memory_space=pl.ANY))
    if prior is not None:
        operands.append(prior)
        in_specs.append(pl.BlockSpec(memory_space=pl.ANY))
        aliases = {len(operands) - 1: 0}
    return pl.pallas_call(
        functools.partial(project_kernel, groups, batch, first),
        grid=(count // step,),
        in_specs=in_specs,
        out_specs=pl.BlockSpec((step, degrees, names), lambda g: (g + lead, 0, 0)),
        out_shape=jax.ShapeDtypeStruct((slab, degrees, names), jnp.float32),
        scratch_shapes=[pltpu.VMEM((step, 2 * batch, groups, inner, depth), jnp.bfloat16)],
        input_output_aliases=aliases,
        compiler_params=pltpu.CompilerParams(vmem_limit_bytes=VMEM_LIMIT),
        cost_estimate=SMALL,
        name="project",
    )(*operands)


def shards(slabs, groups, fields, table):
    batch, band, chans, nlon = fields.shape
    slab, degrees, depth = table.shape
    chips = slabs // 2
    lat, ch = lax.axis_index("lat").astype(jnp.int32), lax.axis_index("ch").astype(jnp.int32)
    me = lat.reshape(1)
    where = jnp.stack([lat % 2, lat // 2])
    south = (me >= chips).astype(jnp.int32)
    info = jnp.stack([ch, (ch * degrees + lat * slab) % 2])
    chunks = split_orders(slab)
    tables = [fourier_rows(nlon, slabs, slab, chunk) for chunk in chunks]
    bits = [1 << k for k in range(groups.bit_length() - 1)]

    def send(block, d):
        return lax.ppermute(block, "lat", xor_pairs(slabs, 2 * d))

    def pass_on(block, bit):
        return lax.ppermute(block, "ch", xor_pairs(groups, bit))

    own = reorder(fields, south)
    other = lax.ppermute(own, "lat", xor_pairs(slabs, 1))
    counts = [2 * count for _, count in chunks]
    total, out = len(chunks), None

    def orders(q, blocks, sources, after):
        return parity(blocks, tuple(sources), chunks[q][1], me, slabs, batch, chans, band, after)

    alone = tuple((d, 0, 1) for d in range(chips))
    near = dft([own], tables[0], counts[:1], alone, where, me, 0, 2)
    sends = dft([other], tables[0], counts[:1], alone, where, me, 1, 2, near)
    if groups != 4 or total != 4 or chips != 4:
        last = me
        for q, (first, count) in enumerate(chunks):
            if q:
                sends = dft([own, other], tables[q], counts[q : q + 1], alone, where, last)
            blocks = [sends[0]] + [send(sends[d], d) for d in range(1, chips)]
            last = orders(q, blocks, [(d, 0) for d in range(chips)], last)
            parts = [last]
            for bit in bits:
                parts += [pass_on(part, bit) for part in parts]
            out = project(table, parts, [0] * groups, count, info, first, batch, 2 * chans, out, last)
        return out

    layout = ((1, 0, 3),) + tuple((d, q, q + 1) for q in range(3) for d in (0, 2, 3))
    rest = dft([own, other], np.concatenate(tables[1:], axis=2), counts[1:], layout, where, sends[0])
    beside = send(rest[0], 1)
    later = [rest[1 + 3 * q : 4 + 3 * q] for q in range(3)]
    parts, pieces = [], []

    def spread(mine):
        parts.append({0: mine, 1: pass_on(mine, 1), 2: pass_on(mine, 2)})

    def forward(q, after):
        have = parts[q]
        one, two = (1, 2) if q % 2 == 0 else (2, 1)
        count = chunks[q][1]
        if q < total - 1:
            (have[one],) = held = gate([have[one]], [have[two], after])
            pieces.append([(0, count, pass_on(held[0], two))])
        else:
            half = count // 2
            held = gate([have[one][:half], have[two][half:]], [after])
            pieces.append([(0, half, pass_on(held[0], two)), (half, count - half, pass_on(held[1], one))])
        return held[0]

    def finish(q, prior, after):
        for start, count, piece in pieces[q]:
            arrays = [parts[q][0], parts[q][1], parts[q][2], piece]
            begins = [start, start, start, 0]
            prior = project(table, arrays, begins, count, info, chunks[q][0] + start, batch, 2 * chans, prior, after)
            after = None
        return prior

    def arrive(q, after):
        blocks = arrived[q]
        if q + 1 < total:
            stay, *leave = later[q]
            held = gate(leave, [*blocks[1:], after])
            arrived.append([stay, send(held[0], 2), send(held[1], 3)])
            after = held[0]
        if q == 0:
            mine = orders(q, blocks, [(d, 0) for d in range(4)], after)
        else:
            skip = sum(counts[1:q])
            mine = orders(q, [*blocks, beside], [(0, 0), (2, 0), (3, 0), (1, skip)], after)
        spread(mine)
        return mine

    arrived = [[sends[0]] + [send(sends[d], d) for d in range(1, 4)]]
    last = arrive(0, rest[0])
    last = arrive(1, last)
    last = forward(0, last)
    last = arrive(2, last)
    last = out = finish(0, out, last)
    last = forward(1, last)
    last = out = finish(1, out, last)
    last = forward(2, last)
    last = arrive(3, last)
    last = forward(3, last)
    out = finish(2, out, last)
    return finish(3, out, None)


def solution(mesh):
    return jax.shard_map(
        functools.partial(shards, mesh.shape["lat"], mesh.shape["ch"]),
        mesh=mesh,
        in_specs=(P(None, "lat", "ch", None), P("lat", "ch", None)),
        out_specs=P("lat", "ch", None),
        check_vma=False,
    )
```

```python
import functools
import math

import jax
import jax.numpy as jnp
import ml_dtypes
import numpy as np
from jax import lax
from jax.experimental import pallas as pl
from jax.experimental.pallas import tpu as pltpu
from jax.sharding import PartitionSpec as P

LANES = 128
SHARES = (2 / 11, 4 / 11, 8 / 11, 1)
VMEM_LIMIT = 60 * 1024 * 1024
SMALL = pl.CostEstimate(flops=1, bytes_accessed=1, transcendentals=0)
NT = (((1,), (1,)), ((), ()))


def fourier_rows(nlon, slabs, slab, chunk):
    first, count = chunk
    orders = (np.arange(slabs)[:, None] * slab + first + np.arange(count)[None, :]).astype(np.int32)
    cols = np.arange(nlon, dtype=np.int32)
    phase = (orders[:, :, None] * cols % nlon).astype(np.float32) * np.float32(2.0 * math.pi / nlon)
    factor = np.float32(1.0 / math.sqrt(nlon))
    rows = np.stack([np.cos(phase) * factor, -np.sin(phase) * factor], axis=1)
    rows = rows.astype(np.float32).astype(ml_dtypes.bfloat16).reshape(slabs // 2, 2, 2 * count, nlon)
    return np.pad(rows.transpose(1, 0, 2, 3), [(0, 0)] * 3 + [(0, -nlon % LANES)])


def reorder_groups(rows, chans):
    step = max(8, 256 // chans // 8 * 8)
    return [(k, min(step, rows - k)) for k in range(0, rows, step)]


def reorder_matrices(count, chans):
    out = np.zeros((2, chans, count, count, chans), np.float32)
    for c in range(chans):
        for k in range(count):
            out[0, c, k, k, c] = 1
            out[1, c, k, count - 1 - k, c] = 1
    return out.reshape(2, chans * count, count * chans).astype(ml_dtypes.bfloat16)


def split_orders(slab):
    if slab % 8:
        return [(0, slab)]
    units = slab // 8
    ends = [round(units * share) for share in SHARES]
    return [(8 * lo, 8 * (hi - lo)) for lo, hi in zip([0] + ends, ends) if hi > lo]


def xor_pairs(size, step):
    return [(i, i ^ step) for i in range(size)]


def reorder_kernel(rows, chans, south_ref, fields_ref, *refs):
    picks, out_ref = refs[:-1], refs[-1]
    south = south_ref[0]
    for (k, count), pick in zip(reorder_groups(rows, chans), picks):
        start = jnp.where(south == 1, rows - k - count, k) * chans
        block = fields_ref[0, pl.ds(pl.multiple_of(start, 8 * chans), count * chans), :]
        res = jnp.dot(pick[0], block, preferred_element_type=jnp.float32).astype(out_ref.dtype)
        for c in range(chans):
            out_ref[0, c * rows + k : c * rows + k + count, : res.shape[1]] = res[c * count : (c + 1) * count]
    blank = out_ref.shape[2] - fields_ref.shape[2]
    if blank:
        out_ref[0, :, fields_ref.shape[2] :] = jnp.zeros((rows * chans, blank), out_ref.dtype)


def reorder(fields, south):
    batch, rows, chans, nlon = fields.shape
    flat, padded = rows * chans, -(-nlon // LANES) * LANES
    picks = [jnp.asarray(reorder_matrices(count, chans)) for _, count in reorder_groups(rows, chans)]
    out = pl.pallas_call(
        functools.partial(reorder_kernel, rows, chans),
        grid_spec=pltpu.PrefetchScalarGridSpec(
            num_scalar_prefetch=1,
            grid=(batch,),
            in_specs=[pl.BlockSpec((1, flat, nlon), lambda b, south: (b, 0, 0))]
            + [pl.BlockSpec((1,) + p.shape[1:], lambda b, south: (south[0], 0, 0)) for p in picks],
            out_specs=pl.BlockSpec((1, flat, padded), lambda b, south: (b, 0, 0)),
        ),
        out_shape=jax.ShapeDtypeStruct((batch, flat, padded), fields.dtype),
        compiler_params=pltpu.CompilerParams(vmem_limit_bytes=VMEM_LIMIT),
        cost_estimate=SMALL,
        name="reorder",
    )(south, fields.reshape(batch, flat, nlon), *picks)
    return out.reshape(batch * flat, padded)


def dft_kernel(chips, counts, layout, bands, where_ref, rows_ref, *refs):
    fields, outs, lhs = refs[:bands], refs[-1 - len(layout) : -1], refs[-1]
    chip = where_ref[1]
    total = sum(counts)
    width = fields[0].shape[0]
    firsts = np.cumsum([0] + list(counts))
    aligned = all(n % 16 == 0 for n in counts)
    for d in range(chips):
        if aligned:
            lhs[d * total : (d + 1) * total] = rows_ref[0, chip ^ d]
    for j in range(bands):
        for n0 in range(0, width, 256):
            cols = slice(n0, min(n0 + 256, width))
            block = fields[j][cols, :]
            if aligned:
                res = lax.dot_general(lhs[...], block, NT, preferred_element_type=jnp.float32)
            for out, (d, lo, hi) in zip(outs, layout):
                if aligned:
                    part = res[d * total + firsts[lo] : d * total + firsts[hi]]
                else:
                    part = lax.dot_general(rows_ref[0, chip ^ d], block, NT, preferred_element_type=jnp.float32)
                out[j, :, cols] = part.astype(jnp.bfloat16)


def dft(flats, rows, counts, layout, where, after, band=0, whole=0, prior=()):
    _, chips, total, nlon = rows.shape
    width = flats[0].shape[0]
    bands = len(flats)
    operands = [where, jnp.asarray(rows), *flats, after, *prior]
    anywhere = pl.BlockSpec(memory_space=pl.ANY)
    sizes = [sum(counts[lo:hi]) for _, lo, hi in layout]
    return pl.pallas_call(
        functools.partial(dft_kernel, chips, counts, layout, bands),
        grid_spec=pltpu.PrefetchScalarGridSpec(
            num_scalar_prefetch=1,
            grid=(1,),
            in_specs=[pl.BlockSpec((1, chips, total, nlon), lambda g, where: (where[0], 0, 0, 0))]
            + [pl.BlockSpec((width, nlon), lambda g, where: (0, 0))] * bands
            + [anywhere] * (1 + len(prior)),
            out_specs=[pl.BlockSpec((bands, n, width), lambda g, where: (band, 0, 0)) for n in sizes],
            scratch_shapes=[pltpu.VMEM((chips * total, nlon), jnp.bfloat16)],
        ),
        out_shape=[jax.ShapeDtypeStruct((whole or bands, n, width), jnp.bfloat16) for n in sizes],
        input_output_aliases={3 + bands + i: i for i in range(len(prior))},
        compiler_params=pltpu.CompilerParams(vmem_limit_bytes=VMEM_LIMIT),
        cost_estimate=SMALL,
        name="dft",
    )(*operands)


def gate(arrays, after):
    anywhere = pl.BlockSpec(memory_space=pl.ANY)
    return pl.pallas_call(
        lambda *refs: None,
        in_specs=[anywhere] * (len(arrays) + len(after)),
        out_specs=[anywhere] * len(arrays),
        out_shape=[jax.ShapeDtypeStruct(a.shape, a.dtype) for a in arrays],
        input_output_aliases={i: i for i in range(len(arrays))},
        cost_estimate=SMALL,
        name="gate",
    )(*arrays, *after)


def packs(names, depth):
    return names % 64 == 0 and depth % LANES == 96


def packed_rows(names, depth):
    tiles = -(-depth // LANES)
    return names * depth // LANES if packs(names, depth) else names * tiles


def parity_kernel(slabs, sources, count, batch, chans, band, me_ref, *refs):
    xs, (_, out_ref, held, *turned) = refs[: len(sources)], refs[len(sources) :]
    me = me_ref[0]
    names = 4 * batch * chans
    depth = band * slabs // 2
    for x, (chip, start) in zip(xs, sources):
        for j in range(2):
            held[me ^ (2 * chip + j)] = x[j, start : start + 2 * count].astype(jnp.float32)
    for i in range(slabs // 2):
        north, south = held[i], held[slabs - 1 - i]
        held[i] = north + south
        held[slabs - 1 - i] = north - south
    for r in range(2):
        orders = slice(r * count, (r + 1) * count)
        for bc in range(batch * chans):
            lanes = slice(bc * band, (bc + 1) * band)
            for s in range(2):
                bands = [i if s == 0 else slabs - 1 - i for i in range(slabs // 2)]
                line = jnp.concatenate([held[i, orders, lanes] for i in bands], axis=1)
                name = (s * batch * chans + bc) * 2 + r
                for t, tile in enumerate(turned):
                    piece = line[:, t * LANES : min((t + 1) * LANES, depth)]
                    if piece.shape[1] < LANES:
                        blank = jnp.zeros((count, LANES - piece.shape[1]), jnp.float32)
                        piece = jnp.concatenate([piece, blank], axis=1)
                    tile[pl.ds(name, count, stride=names), :] = piece
    packed = packs(names, depth)

    def write(m, carry):
        rows = pl.ds(pl.multiple_of(m * names, names), names)
        for t, tile in enumerate(turned):
            block = tile[rows, :].astype(jnp.bfloat16)
            if packed and t == len(turned) - 1:
                step = names // 4
                last = block[3 * step :]
                for g in range(3):
                    both = jnp.concatenate(
                        [block[g * step : (g + 1) * step, :96], last[:, 32 * g : 32 * (g + 1)]], axis=1
                    )
                    out_ref[m, t * names + g * step : t * names + (g + 1) * step, :] = both
            else:
                out_ref[m, t * names : (t + 1) * names, :] = block
        return carry

    lax.fori_loop(0, count, write, 0)


def parity(blocks, sources, count, me, slabs, batch, chans, band, after):
    width = blocks[0].shape[2]
    names = 4 * batch * chans
    depth = band * slabs // 2
    total = packed_rows(names, depth)
    return pl.pallas_call(
        functools.partial(parity_kernel, slabs, sources, count, batch, chans, band),
        grid=(1,),
        in_specs=[pl.BlockSpec(memory_space=pltpu.SMEM)]
        + [pl.BlockSpec(block.shape, lambda g: (0, 0, 0)) for block in blocks]
        + [pl.BlockSpec(memory_space=pl.ANY)],
        out_specs=pl.BlockSpec((count, total, LANES), lambda g: (0, 0, 0)),
        out_shape=jax.ShapeDtypeStruct((count, total, LANES), jnp.bfloat16),
        scratch_shapes=[pltpu.VMEM((slabs, 2 * count, width), jnp.float32)]
        + [pltpu.VMEM((count * names, LANES), jnp.float32)] * -(-depth // LANES),
        compiler_params=pltpu.CompilerParams(vmem_limit_bytes=VMEM_LIMIT),
        cost_estimate=SMALL,
        name="parity",
    )(me, *blocks, after)


def project_kernel(groups, batch, first, gathered, info_ref, table_ref, *refs):
    parts, out_ref, rhs = refs[:groups], refs[-2], refs[-1]
    me, odd = info_ref[0], info_ref[1]
    orders, degrees, depth = table_ref.shape
    inner = rhs.shape[3]
    names = 2 * batch * inner
    packed = packs(names, depth)
    tiles = -(-depth // LANES)
    for m in range(orders):
        for d in range(groups):
            ch = d if gathered else me ^ d
            for sb in range(2 * batch):
                for t in range(tiles):
                    width = min(LANES, depth - t * LANES)
                    base = t * names
                    if packed and t == tiles - 1:
                        step = names // 4
                        if (sb + 1) * inner <= 3 * step:
                            block = parts[d][m, base + sb * inner : base + (sb + 1) * inner, :width]
                        else:
                            off = sb * inner - 3 * step
                            block = jnp.concatenate(
                                [
                                    parts[d][m, base + g * step + off : base + g * step + off + inner, 96:]
                                    for g in range(3)
                                ],
                                axis=1,
                            )
                    else:
                        block = parts[d][m, base + sb * inner : base + (sb + 1) * inner, :width]
                    rhs[m, sb, ch, :, t * LANES : t * LANES + width] = block
    row = lax.broadcasted_iota(jnp.int32, (degrees, batch * groups * inner), 0)
    start = pl.program_id(0) * orders + first
    for m in range(orders):
        right = rhs[m].reshape(2 * batch * groups * inner, depth)
        both = lax.dot_general(table_ref[m], right, NT, preferred_element_type=jnp.float32)
        cut = batch * groups * inner
        even = ((row + (odd + start + m)) & 1) == 0
        out_ref[m] = jnp.where(even, both[:, :cut], both[:, cut:])


def project(table, parts, starts, count, info, first, batch, inner, prior, after):
    slab, degrees, depth = table.shape
    groups = len(parts)
    gathered = parts[0].ndim == 4
    total = parts[0].shape[-2]
    step = 4 if count % 4 == 0 and first % 4 == 0 else count
    lead = first // step
    names = batch * groups * inner
    operands = [info, table, *parts]
    in_specs = [
        pl.BlockSpec(memory_space=pltpu.SMEM),
        pl.BlockSpec((step, degrees, depth), lambda g: (g + lead, 0, 0)),
    ]
    for d, start in enumerate(starts):
        if gathered:
            in_specs.append(pl.BlockSpec((None, step, total, LANES), functools.partial(lambda d, g: (d, g, 0, 0), d)))
        else:
            skip = start // step
            in_specs.append(pl.BlockSpec((step, total, LANES), functools.partial(lambda skip, g: (g + skip, 0, 0), skip)))
    aliases = {}
    if after is not None:
        operands.append(after)
        in_specs.append(pl.BlockSpec(memory_space=pl.ANY))
    if prior is not None:
        operands.append(prior)
        in_specs.append(pl.BlockSpec(memory_space=pl.ANY))
        aliases = {len(operands) - 1: 0}
    return pl.pallas_call(
        functools.partial(project_kernel, groups, batch, first, gathered),
        grid=(count // step,),
        in_specs=in_specs,
        out_specs=pl.BlockSpec((step, degrees, names), lambda g: (g + lead, 0, 0)),
        out_shape=jax.ShapeDtypeStruct((slab, degrees, names), jnp.float32),
        scratch_shapes=[pltpu.VMEM((step, 2 * batch, groups, inner, depth), jnp.bfloat16)],
        input_output_aliases=aliases,
        compiler_params=pltpu.CompilerParams(vmem_limit_bytes=VMEM_LIMIT),
        cost_estimate=SMALL,
        name="project",
    )(*operands)


def shards(slabs, groups, fields, table):
    batch, band, chans, nlon = fields.shape
    slab, degrees, depth = table.shape
    chips = slabs // 2
    lat, ch = lax.axis_index("lat").astype(jnp.int32), lax.axis_index("ch").astype(jnp.int32)
    me = lat.reshape(1)
    where = jnp.stack([lat % 2, lat // 2])
    south = (me >= chips).astype(jnp.int32)
    info = jnp.stack([ch, (ch * degrees + lat * slab) % 2])
    chunks = split_orders(slab)
    tables = [fourier_rows(nlon, slabs, slab, chunk) for chunk in chunks]
    bits = [1 << k for k in range(groups.bit_length() - 1)]

    def send(block, d):
        return lax.ppermute(block, "lat", xor_pairs(slabs, 2 * d))

    def pass_on(block, bit):
        return lax.ppermute(block, "ch", xor_pairs(groups, bit))

    own = reorder(fields, south)
    other = lax.ppermute(own, "lat", xor_pairs(slabs, 1))
    counts = [2 * count for _, count in chunks]
    total, out = len(chunks), None

    def orders(q, blocks, sources, after):
        return parity(blocks, tuple(sources), chunks[q][1], me, slabs, batch, chans, band, after)

    alone = tuple((d, 0, 1) for d in range(chips))
    near = dft([own], tables[0], counts[:1], alone, where, me, 0, 2)
    sends = dft([other], tables[0], counts[:1], alone, where, me, 1, 2, near)
    if groups != 4 or total != 4 or chips != 4:
        last = me
        for q, (first, count) in enumerate(chunks):
            if q:
                sends = dft([own, other], tables[q], counts[q : q + 1], alone, where, last)
            blocks = [sends[0]] + [send(sends[d], d) for d in range(1, chips)]
            last = orders(q, blocks, [(d, 0) for d in range(chips)], last)
            parts = [last]
            for bit in bits:
                parts += [pass_on(part, bit) for part in parts]
            out = project(table, parts, [0] * groups, count, info, first, batch, 2 * chans, out, last)
        return out

    layout = ((1, 0, 3),) + tuple((d, q, q + 1) for q in range(3) for d in (0, 2, 3))
    rest = dft([own, other], np.concatenate(tables[1:], axis=2), counts[1:], layout, where, sends[0])
    beside = send(rest[0], 1)
    later = [rest[1 + 3 * q : 4 + 3 * q] for q in range(3)]
    parts, pieces = {}, {}

    def spread(q, mine):
        if q % 2 == 0:
            parts[q] = lax.all_gather(mine, "ch")
        else:
            parts[q] = {0: mine, 1: pass_on(mine, 1), 2: pass_on(mine, 2)}

    def forward(q, after):
        have = parts[q]
        half = chunks[q][1] // 2
        held = gate([have[1][:half], have[2][half:]], [after])
        pieces[q] = [(0, half, pass_on(held[0], 2)), (half, half, pass_on(held[1], 1))]
        return held[0]

    def finish(q, prior, after):
        first, count = chunks[q]
        if q % 2 == 0:
            return project(table, [parts[q]] * 4, [0] * 4, count, info, first, batch, 2 * chans, prior, after)
        for start, count, piece in pieces[q]:
            arrays = [parts[q][0], parts[q][1], parts[q][2], piece]
            begins = [start, start, start, 0]
            prior = project(table, arrays, begins, count, info, first + start, batch, 2 * chans, prior, after)
            after = None
        return prior

    def arrive(q, after):
        blocks = arrived[q]
        if q + 1 < total:
            stay, *leave = later[q]
            held = gate(leave, [*blocks[1:], after])
            arrived.append([stay, send(held[0], 2), send(held[1], 3)])
            after = held[0]
        if q == 0:
            mine = orders(q, blocks, [(d, 0) for d in range(4)], after)
        else:
            skip = sum(counts[1:q])
            mine = orders(q, [*blocks, beside], [(0, 0), (2, 0), (3, 0), (1, skip)], after)
        spread(q, mine)
        return mine

    arrived = [[sends[0]] + [send(sends[d], d) for d in range(1, 4)]]
    last = arrive(0, rest[0])
    last = arrive(1, last)
    last = forward(1, last)
    last = arrive(2, last)
    out = finish(0, out, last)
    last = out = finish(1, out, None)
    last = arrive(3, last)
    last = forward(3, last)
    out = finish(2, out, last)
    return finish(3, out, None)


def solution(mesh):
    return jax.shard_map(
        functools.partial(shards, mesh.shape["lat"], mesh.shape["ch"]),
        mesh=mesh,
        in_specs=(P(None, "lat", "ch", None), P("lat", "ch", None)),
        out_specs=P("lat", "ch", None),
        check_vma=False,
    )
```

```python
import functools
import math

import jax
import jax.numpy as jnp
import ml_dtypes
import numpy as np
from jax import lax
from jax.experimental import pallas as pl
from jax.experimental.pallas import tpu as pltpu
from jax.sharding import PartitionSpec as P

LANES = 128
SHARES = (2 / 11, 6 / 11, 1)
VMEM_LIMIT = 60 * 1024 * 1024


def cost(micros):
    return pl.CostEstimate(flops=0, bytes_accessed=int(micros * 3.69e6), transcendentals=0)


NT = (((1,), (1,)), ((), ()))


def fourier_rows(nlon, slabs, slab, chunk):
    first, count = chunk
    orders = (np.arange(slabs)[:, None] * slab + first + np.arange(count)[None, :]).astype(np.int32)
    cols = np.arange(nlon, dtype=np.int32)
    phase = (orders[:, :, None] * cols % nlon).astype(np.float32) * np.float32(2.0 * math.pi / nlon)
    factor = np.float32(1.0 / math.sqrt(nlon))
    rows = np.stack([np.cos(phase) * factor, -np.sin(phase) * factor], axis=1)
    rows = rows.astype(np.float32).astype(ml_dtypes.bfloat16).reshape(slabs // 2, 2, 2 * count, nlon)
    return np.pad(rows.transpose(1, 0, 2, 3), [(0, 0)] * 3 + [(0, -nlon % LANES)])


def reorder_groups(rows, chans):
    step = max(8, 256 // chans // 8 * 8)
    return [(k, min(step, rows - k)) for k in range(0, rows, step)]


def reorder_matrices(count, chans):
    out = np.zeros((2, chans, count, count, chans), np.float32)
    for c in range(chans):
        for k in range(count):
            out[0, c, k, k, c] = 1
            out[1, c, k, count - 1 - k, c] = 1
    return out.reshape(2, chans * count, count * chans).astype(ml_dtypes.bfloat16)


def split_orders(slab):
    if slab % 8:
        return [(0, slab)]
    units = slab // 8
    ends = [round(units * share) for share in SHARES]
    return [(8 * lo, 8 * (hi - lo)) for lo, hi in zip([0] + ends, ends) if hi > lo]


def xor_pairs(size, step):
    return [(i, i ^ step) for i in range(size)]


def reorder_kernel(rows, chans, south_ref, fields_ref, *refs):
    picks, out_ref = refs[:-1], refs[-1]
    south = south_ref[0]
    for (k, count), pick in zip(reorder_groups(rows, chans), picks):
        start = jnp.where(south == 1, rows - k - count, k) * chans
        block = fields_ref[0, pl.ds(pl.multiple_of(start, 8 * chans), count * chans), :]
        res = jnp.dot(pick[0], block, preferred_element_type=jnp.float32).astype(out_ref.dtype)
        for c in range(chans):
            out_ref[0, c * rows + k : c * rows + k + count, : res.shape[1]] = res[c * count : (c + 1) * count]
    blank = out_ref.shape[2] - fields_ref.shape[2]
    if blank:
        out_ref[0, :, fields_ref.shape[2] :] = jnp.zeros((rows * chans, blank), out_ref.dtype)


def reorder(fields, south):
    batch, rows, chans, nlon = fields.shape
    flat, padded = rows * chans, -(-nlon // LANES) * LANES
    picks = [jnp.asarray(reorder_matrices(count, chans)) for _, count in reorder_groups(rows, chans)]
    out = pl.pallas_call(
        functools.partial(reorder_kernel, rows, chans),
        grid_spec=pltpu.PrefetchScalarGridSpec(
            num_scalar_prefetch=1,
            grid=(batch,),
            in_specs=[pl.BlockSpec((1, flat, nlon), lambda b, south: (b, 0, 0))]
            + [pl.BlockSpec((1,) + p.shape[1:], lambda b, south: (south[0], 0, 0)) for p in picks],
            out_specs=pl.BlockSpec((1, flat, padded), lambda b, south: (b, 0, 0)),
        ),
        out_shape=jax.ShapeDtypeStruct((batch, flat, padded), fields.dtype),
        compiler_params=pltpu.CompilerParams(vmem_limit_bytes=VMEM_LIMIT),
        cost_estimate=cost(5),
        name="reorder",
    )(south, fields.reshape(batch, flat, nlon), *picks)
    return out.reshape(batch * flat, padded)


def dft_kernel(chips, counts, layout, bands, where_ref, rows_ref, *refs):
    fields, outs, lhs = refs[:bands], refs[-1 - len(layout) : -1], refs[-1]
    chip = where_ref[1]
    total = sum(counts)
    width = fields[0].shape[0]
    firsts = np.cumsum([0] + list(counts))
    aligned = all(n % 16 == 0 for n in counts)
    for d in range(chips):
        if aligned:
            lhs[d * total : (d + 1) * total] = rows_ref[0, chip ^ d]
    for j in range(bands):
        for n0 in range(0, width, 256):
            cols = slice(n0, min(n0 + 256, width))
            block = fields[j][cols, :]
            if aligned:
                res = lax.dot_general(lhs[...], block, NT, preferred_element_type=jnp.float32)
            for out, (d, lo, hi) in zip(outs, layout):
                if aligned:
                    part = res[d * total + firsts[lo] : d * total + firsts[hi]]
                else:
                    part = lax.dot_general(rows_ref[0, chip ^ d], block, NT, preferred_element_type=jnp.float32)
                out[j, :, cols] = part.astype(jnp.bfloat16)


def dft(flats, rows, counts, layout, where, after, band=0, whole=0, prior=()):
    _, chips, total, nlon = rows.shape
    width = flats[0].shape[0]
    bands = len(flats)
    operands = [where, jnp.asarray(rows), *flats, after, *prior]
    anywhere = pl.BlockSpec(memory_space=pl.ANY)
    sizes = [sum(counts[lo:hi]) for _, lo, hi in layout]
    return pl.pallas_call(
        functools.partial(dft_kernel, chips, counts, layout, bands),
        grid_spec=pltpu.PrefetchScalarGridSpec(
            num_scalar_prefetch=1,
            grid=(1,),
            in_specs=[pl.BlockSpec((1, chips, total, nlon), lambda g, where: (where[0], 0, 0, 0))]
            + [pl.BlockSpec((width, nlon), lambda g, where: (0, 0))] * bands
            + [anywhere] * (1 + len(prior)),
            out_specs=[pl.BlockSpec((bands, n, width), lambda g, where: (band, 0, 0)) for n in sizes],
            scratch_shapes=[pltpu.VMEM((chips * total, nlon), jnp.bfloat16)],
        ),
        out_shape=[jax.ShapeDtypeStruct((whole or bands, n, width), jnp.bfloat16) for n in sizes],
        input_output_aliases={3 + bands + i: i for i in range(len(prior))},
        compiler_params=pltpu.CompilerParams(vmem_limit_bytes=VMEM_LIMIT),
        cost_estimate=cost(sum(counts) * bands / 24),
        name="dft",
    )(*operands)


def gate(arrays, after):
    anywhere = pl.BlockSpec(memory_space=pl.ANY)
    return pl.pallas_call(
        lambda *refs: None,
        in_specs=[anywhere] * (len(arrays) + len(after)),
        out_specs=[anywhere] * len(arrays),
        out_shape=[jax.ShapeDtypeStruct(a.shape, a.dtype) for a in arrays],
        input_output_aliases={i: i for i in range(len(arrays))},
        cost_estimate=cost(0),
        name="gate",
    )(*arrays, *after)


def packs(names, depth):
    return names % 64 == 0 and depth % LANES == 96


def packed_rows(names, depth):
    tiles = -(-depth // LANES)
    return names * depth // LANES if packs(names, depth) else names * tiles


def parity_kernel(slabs, sources, count, batch, chans, band, me_ref, *refs):
    xs, (_, out_ref, held, *turned) = refs[: len(sources)], refs[len(sources) :]
    me = me_ref[0]
    names = 4 * batch * chans
    depth = band * slabs // 2
    for x, (chip, start) in zip(xs, sources):
        for j in range(2):
            held[me ^ (2 * chip + j)] = x[j, start : start + 2 * count].astype(jnp.float32)
    for i in range(slabs // 2):
        north, south = held[i], held[slabs - 1 - i]
        held[i] = north + south
        held[slabs - 1 - i] = north - south
    for r in range(2):
        orders = slice(r * count, (r + 1) * count)
        for bc in range(batch * chans):
            lanes = slice(bc * band, (bc + 1) * band)
            for s in range(2):
                bands = [i if s == 0 else slabs - 1 - i for i in range(slabs // 2)]
                line = jnp.concatenate([held[i, orders, lanes] for i in bands], axis=1)
                name = (s * batch * chans + bc) * 2 + r
                for t, tile in enumerate(turned):
                    piece = line[:, t * LANES : min((t + 1) * LANES, depth)]
                    if piece.shape[1] < LANES:
                        blank = jnp.zeros((count, LANES - piece.shape[1]), jnp.float32)
                        piece = jnp.concatenate([piece, blank], axis=1)
                    tile[pl.ds(name, count, stride=names), :] = piece
    packed = packs(names, depth)

    def write(m, carry):
        rows = pl.ds(pl.multiple_of(m * names, names), names)
        for t, tile in enumerate(turned):
            block = tile[rows, :].astype(jnp.bfloat16)
            if packed and t == len(turned) - 1:
                step = names // 4
                last = block[3 * step :]
                for g in range(3):
                    both = jnp.concatenate(
                        [block[g * step : (g + 1) * step, :96], last[:, 32 * g : 32 * (g + 1)]], axis=1
                    )
                    out_ref[m, t * names + g * step : t * names + (g + 1) * step, :] = both
            else:
                out_ref[m, t * names : (t + 1) * names, :] = block
        return carry

    lax.fori_loop(0, count, write, 0)


def parity(blocks, sources, count, me, slabs, batch, chans, band, after):
    width = blocks[0].shape[2]
    names = 4 * batch * chans
    depth = band * slabs // 2
    total = packed_rows(names, depth)
    return pl.pallas_call(
        functools.partial(parity_kernel, slabs, sources, count, batch, chans, band),
        grid=(1,),
        in_specs=[pl.BlockSpec(memory_space=pltpu.SMEM)]
        + [pl.BlockSpec(block.shape, lambda g: (0, 0, 0)) for block in blocks]
        + [pl.BlockSpec(memory_space=pl.ANY)],
        out_specs=pl.BlockSpec((count, total, LANES), lambda g: (0, 0, 0)),
        out_shape=jax.ShapeDtypeStruct((count, total, LANES), jnp.bfloat16),
        scratch_shapes=[pltpu.VMEM((slabs, 2 * count, width), jnp.float32)]
        + [pltpu.VMEM((count * names, LANES), jnp.float32)] * -(-depth // LANES),
        compiler_params=pltpu.CompilerParams(vmem_limit_bytes=VMEM_LIMIT),
        cost_estimate=cost(count),
        name="parity",
    )(me, *blocks, after)


def project_kernel(groups, batch, first, info_ref, table_ref, *refs):
    parts, out_ref, rhs = refs[:groups], refs[-2], refs[-1]
    me, odd = info_ref[0], info_ref[1]
    orders, degrees, depth = table_ref.shape
    inner = rhs.shape[3]
    names = 2 * batch * inner
    packed = packs(names, depth)
    tiles = -(-depth // LANES)
    for m in range(orders):
        for d in range(groups):
            ch = me ^ d
            for sb in range(2 * batch):
                for t in range(tiles):
                    width = min(LANES, depth - t * LANES)
                    base = t * names
                    if packed and t == tiles - 1:
                        step = names // 4
                        if (sb + 1) * inner <= 3 * step:
                            block = parts[d][m, base + sb * inner : base + (sb + 1) * inner, :width]
                        else:
                            off = sb * inner - 3 * step
                            block = jnp.concatenate(
                                [
                                    parts[d][m, base + g * step + off : base + g * step + off + inner, 96:]
                                    for g in range(3)
                                ],
                                axis=1,
                            )
                    else:
                        block = parts[d][m, base + sb * inner : base + (sb + 1) * inner, :width]
                    rhs[m, sb, ch, :, t * LANES : t * LANES + width] = block
    row = lax.broadcasted_iota(jnp.int32, (degrees, batch * groups * inner), 0)
    start = pl.program_id(0) * orders + first
    for m in range(orders):
        right = rhs[m].reshape(2 * batch * groups * inner, depth)
        both = lax.dot_general(table_ref[m], right, NT, preferred_element_type=jnp.float32)
        cut = batch * groups * inner
        even = ((row + (odd + start + m)) & 1) == 0
        out_ref[m] = jnp.where(even, both[:, :cut], both[:, cut:])


def project(table, parts, starts, count, info, first, batch, inner, prior, after):
    slab, degrees, depth = table.shape
    groups = len(parts)
    total = parts[0].shape[1]
    step = 4 if count % 4 == 0 and first % 4 == 0 else count
    lead = first // step
    names = batch * groups * inner
    operands = [info, table, *parts]
    in_specs = [
        pl.BlockSpec(memory_space=pltpu.SMEM),
        pl.BlockSpec((step, degrees, depth), lambda g: (g + lead, 0, 0)),
    ] + [
        pl.BlockSpec((step, total, LANES), functools.partial(lambda skip, g: (g + skip, 0, 0), start // step))
        for start in starts
    ]
    aliases = {}
    if after is not None:
        operands.append(after)
        in_specs.append(pl.BlockSpec(memory_space=pl.ANY))
    if prior is not None:
        operands.append(prior)
        in_specs.append(pl.BlockSpec(memory_space=pl.ANY))
        aliases = {len(operands) - 1: 0}
    return pl.pallas_call(
        functools.partial(project_kernel, groups, batch, first),
        grid=(count // step,),
        in_specs=in_specs,
        out_specs=pl.BlockSpec((step, degrees, names), lambda g: (g + lead, 0, 0)),
        out_shape=jax.ShapeDtypeStruct((slab, degrees, names), jnp.float32),
        scratch_shapes=[pltpu.VMEM((step, 2 * batch, groups, inner, depth), jnp.bfloat16)],
        input_output_aliases=aliases,
        compiler_params=pltpu.CompilerParams(vmem_limit_bytes=VMEM_LIMIT),
        cost_estimate=cost(count / 4),
        name="project",
    )(*operands)


def shards(slabs, groups, fields, table):
    batch, band, chans, nlon = fields.shape
    slab, degrees, depth = table.shape
    chips = slabs // 2
    lat, ch = lax.axis_index("lat").astype(jnp.int32), lax.axis_index("ch").astype(jnp.int32)
    me = lat.reshape(1)
    where = jnp.stack([lat % 2, lat // 2])
    south = (me >= chips).astype(jnp.int32)
    info = jnp.stack([ch, (ch * degrees + lat * slab) % 2])
    chunks = split_orders(slab)
    tables = [fourier_rows(nlon, slabs, slab, chunk) for chunk in chunks]
    bits = [1 << k for k in range(groups.bit_length() - 1)]

    def send(block, d):
        return lax.ppermute(block, "lat", xor_pairs(slabs, 2 * d))

    def pass_on(block, bit):
        return lax.ppermute(block, "ch", xor_pairs(groups, bit))

    own = reorder(fields, south)
    other = lax.ppermute(own, "lat", xor_pairs(slabs, 1))
    counts = [2 * count for _, count in chunks]
    total, out = len(chunks), None

    def orders(q, blocks, sources, after):
        return parity(blocks, tuple(sources), chunks[q][1], me, slabs, batch, chans, band, after)

    alone = tuple((d, 0, 1) for d in range(chips))
    near = dft([own], tables[0], counts[:1], alone, where, me, 0, 2)
    sends = dft([other], tables[0], counts[:1], alone, where, me, 1, 2, near)
    if groups != 4 or total != 3 or chips != 4:
        last = me
        for q, (first, count) in enumerate(chunks):
            if q:
                sends = dft([own, other], tables[q], counts[q : q + 1], alone, where, last)
            blocks = [sends[0]] + [send(sends[d], d) for d in range(1, chips)]
            last = orders(q, blocks, [(d, 0) for d in range(chips)], last)
            parts = [last]
            for bit in bits:
                parts += [pass_on(part, bit) for part in parts]
            out = project(table, parts, [0] * groups, count, info, first, batch, 2 * chans, out, last)
        return out

    layout = ((1, 0, 2),) + tuple((d, q, q + 1) for q in range(2) for d in (0, 2, 3))
    rest = dft([own, other], np.concatenate(tables[1:], axis=2), counts[1:], layout, where, sends[0])
    beside = send(rest[0], 1)
    later = [rest[1 + 3 * q : 4 + 3 * q] for q in range(2)]
    parts, pieces = {}, {}

    def spread(q, mine):
        parts[q] = {0: mine, 1: pass_on(mine, 1), 2: pass_on(mine, 2)}

    def forward(q, after):
        have = parts[q]
        half = chunks[q][1] // 2
        held = gate([have[1][:half], have[2][half:]], [after])
        pieces[q] = [(0, half, pass_on(held[0], 2)), (half, half, pass_on(held[1], 1))]
        return held[0]

    def finish(q, prior, after):
        for start, count, piece in pieces[q]:
            arrays = [parts[q][0], parts[q][1], parts[q][2], piece]
            begins = [start, start, start, 0]
            first = chunks[q][0] + start
            prior = project(table, arrays, begins, count, info, first, batch, 2 * chans, prior, after)
            after = None
        return prior

    def arrive(q, after):
        blocks = arrived[q]
        if q + 1 < total:
            stay, *leave = later[q]
            passed = [piece for _, _, piece in pieces.get(q - 1, [])]
            held = gate(leave, [*blocks[1:], *passed, after])
            arrived.append([stay, send(held[0], 2), send(held[1], 3)])
            after = held[0]
        if q == 0:
            mine = orders(q, blocks, [(d, 0) for d in range(4)], after)
        else:
            skip = sum(counts[1:q])
            mine = orders(q, [*blocks, beside], [(0, 0), (2, 0), (3, 0), (1, skip)], after)
        spread(q, mine)
        return mine

    arrived = [[sends[0]] + [send(sends[d], d) for d in range(1, 4)]]
    last = arrive(0, rest[0])
    last = forward(0, last)
    last = arrive(1, last)
    last = out = finish(0, out, last)
    last = arrive(2, last)
    last = forward(1, last)
    last = out = finish(1, out, last)
    last = forward(2, last)
    return finish(2, out, last)


def solution(mesh):
    return jax.shard_map(
        functools.partial(shards, mesh.shape["lat"], mesh.shape["ch"]),
        mesh=mesh,
        in_specs=(P(None, "lat", "ch", None), P("lat", "ch", None)),
        out_specs=P("lat", "ch", None),
        check_vma=False,
    )
```

```python
import functools
import math

import jax
import jax.numpy as jnp
import ml_dtypes
import numpy as np
from jax import lax
from jax.experimental import pallas as pl
from jax.experimental.pallas import tpu as pltpu
from jax.sharding import PartitionSpec as P

LANES = 128
SHARES = (2 / 11, 6 / 11, 1)
VMEM_LIMIT = 60 * 1024 * 1024


def cost(micros):
    return pl.CostEstimate(flops=0, bytes_accessed=int(micros * 3.69e6), transcendentals=0)


NT = (((1,), (1,)), ((), ()))


def fourier_rows(nlon, slabs, slab, chunk):
    first, count = chunk
    orders = (np.arange(slabs)[:, None] * slab + first + np.arange(count)[None, :]).astype(np.int32)
    cols = np.arange(nlon, dtype=np.int32)
    phase = (orders[:, :, None] * cols % nlon).astype(np.float32) * np.float32(2.0 * math.pi / nlon)
    factor = np.float32(1.0 / math.sqrt(nlon))
    rows = np.stack([np.cos(phase) * factor, -np.sin(phase) * factor], axis=1)
    rows = rows.astype(np.float32).astype(ml_dtypes.bfloat16).reshape(slabs // 2, 2, 2 * count, nlon)
    return np.pad(rows.transpose(1, 0, 2, 3), [(0, 0)] * 3 + [(0, -nlon % LANES)])


def reorder_groups(rows, chans):
    step = max(8, 256 // chans // 8 * 8)
    return [(k, min(step, rows - k)) for k in range(0, rows, step)]


def reorder_matrices(count, chans):
    out = np.zeros((2, chans, count, count, chans), np.float32)
    for c in range(chans):
        for k in range(count):
            out[0, c, k, k, c] = 1
            out[1, c, k, count - 1 - k, c] = 1
    return out.reshape(2, chans * count, count * chans).astype(ml_dtypes.bfloat16)


def split_orders(slab):
    if slab % 8:
        return [(0, slab)]
    units = slab // 8
    ends = [round(units * share) for share in SHARES]
    return [(8 * lo, 8 * (hi - lo)) for lo, hi in zip([0] + ends, ends) if hi > lo]


def xor_pairs(size, step):
    return [(i, i ^ step) for i in range(size)]


def reorder_kernel(rows, chans, south_ref, fields_ref, *refs):
    picks, out_ref = refs[:-1], refs[-1]
    south = south_ref[0]
    for (k, count), pick in zip(reorder_groups(rows, chans), picks):
        start = jnp.where(south == 1, rows - k - count, k) * chans
        block = fields_ref[0, pl.ds(pl.multiple_of(start, 8 * chans), count * chans), :]
        res = jnp.dot(pick[0], block, preferred_element_type=jnp.float32).astype(out_ref.dtype)
        for c in range(chans):
            out_ref[0, c * rows + k : c * rows + k + count, : res.shape[1]] = res[c * count : (c + 1) * count]
    blank = out_ref.shape[2] - fields_ref.shape[2]
    if blank:
        out_ref[0, :, fields_ref.shape[2] :] = jnp.zeros((rows * chans, blank), out_ref.dtype)


def reorder(fields, south):
    batch, rows, chans, nlon = fields.shape
    flat, padded = rows * chans, -(-nlon // LANES) * LANES
    picks = [jnp.asarray(reorder_matrices(count, chans)) for _, count in reorder_groups(rows, chans)]
    out = pl.pallas_call(
        functools.partial(reorder_kernel, rows, chans),
        grid_spec=pltpu.PrefetchScalarGridSpec(
            num_scalar_prefetch=1,
            grid=(batch,),
            in_specs=[pl.BlockSpec((1, flat, nlon), lambda b, south: (b, 0, 0))]
            + [pl.BlockSpec((1,) + p.shape[1:], lambda b, south: (south[0], 0, 0)) for p in picks],
            out_specs=pl.BlockSpec((1, flat, padded), lambda b, south: (b, 0, 0)),
        ),
        out_shape=jax.ShapeDtypeStruct((batch, flat, padded), fields.dtype),
        compiler_params=pltpu.CompilerParams(vmem_limit_bytes=VMEM_LIMIT),
        cost_estimate=cost(5),
        name="reorder",
    )(south, fields.reshape(batch, flat, nlon), *picks)
    return out.reshape(batch * flat, padded)


def dft_kernel(chips, counts, layout, bands, where_ref, rows_ref, *refs):
    fields, outs, lhs = refs[:bands], refs[-1 - len(layout) : -1], refs[-1]
    chip = where_ref[1]
    total = sum(counts)
    width = fields[0].shape[0]
    firsts = np.cumsum([0] + list(counts))
    aligned = all(n % 16 == 0 for n in counts)
    for d in range(chips):
        if aligned:
            lhs[d * total : (d + 1) * total] = rows_ref[0, chip ^ d]
    for j in range(bands):
        for n0 in range(0, width, 256):
            cols = slice(n0, min(n0 + 256, width))
            block = fields[j][cols, :]
            if aligned:
                res = lax.dot_general(lhs[...], block, NT, preferred_element_type=jnp.float32)
            for out, (d, lo, hi) in zip(outs, layout):
                if aligned:
                    part = res[d * total + firsts[lo] : d * total + firsts[hi]]
                else:
                    part = lax.dot_general(rows_ref[0, chip ^ d], block, NT, preferred_element_type=jnp.float32)
                out[j, :, cols] = part.astype(jnp.bfloat16)


def dft(flats, rows, counts, layout, where, after, band=0, whole=0, prior=()):
    _, chips, total, nlon = rows.shape
    width = flats[0].shape[0]
    bands = len(flats)
    operands = [where, jnp.asarray(rows), *flats, after, *prior]
    anywhere = pl.BlockSpec(memory_space=pl.ANY)
    sizes = [sum(counts[lo:hi]) for _, lo, hi in layout]
    return pl.pallas_call(
        functools.partial(dft_kernel, chips, counts, layout, bands),
        grid_spec=pltpu.PrefetchScalarGridSpec(
            num_scalar_prefetch=1,
            grid=(1,),
            in_specs=[pl.BlockSpec((1, chips, total, nlon), lambda g, where: (where[0], 0, 0, 0))]
            + [pl.BlockSpec((width, nlon), lambda g, where: (0, 0))] * bands
            + [anywhere] * (1 + len(prior)),
            out_specs=[pl.BlockSpec((bands, n, width), lambda g, where: (band, 0, 0)) for n in sizes],
            scratch_shapes=[pltpu.VMEM((chips * total, nlon), jnp.bfloat16)],
        ),
        out_shape=[jax.ShapeDtypeStruct((whole or bands, n, width), jnp.bfloat16) for n in sizes],
        input_output_aliases={3 + bands + i: i for i in range(len(prior))},
        compiler_params=pltpu.CompilerParams(vmem_limit_bytes=VMEM_LIMIT),
        cost_estimate=cost(sum(counts) * bands / 24),
        name="dft",
    )(*operands)


def gate(arrays, after):
    anywhere = pl.BlockSpec(memory_space=pl.ANY)
    return pl.pallas_call(
        lambda *refs: None,
        in_specs=[anywhere] * (len(arrays) + len(after)),
        out_specs=[anywhere] * len(arrays),
        out_shape=[jax.ShapeDtypeStruct(a.shape, a.dtype) for a in arrays],
        input_output_aliases={i: i for i in range(len(arrays))},
        cost_estimate=cost(0),
        name="gate",
    )(*arrays, *after)


def packs(names, depth):
    return names % 64 == 0 and depth % LANES == 96


def packed_rows(names, depth):
    tiles = -(-depth // LANES)
    return names * depth // LANES if packs(names, depth) else names * tiles


def parity_kernel(slabs, sources, count, batch, chans, band, me_ref, *refs):
    xs, (_, out_ref, held, *turned) = refs[: len(sources)], refs[len(sources) :]
    me = me_ref[0]
    names = 4 * batch * chans
    depth = band * slabs // 2
    for x, (chip, start) in zip(xs, sources):
        for j in range(2):
            held[me ^ (2 * chip + j)] = x[j, start : start + 2 * count].astype(jnp.float32)
    for i in range(slabs // 2):
        north, south = held[i], held[slabs - 1 - i]
        held[i] = north + south
        held[slabs - 1 - i] = north - south
    for r in range(2):
        orders = slice(r * count, (r + 1) * count)
        for bc in range(batch * chans):
            lanes = slice(bc * band, (bc + 1) * band)
            for s in range(2):
                bands = [i if s == 0 else slabs - 1 - i for i in range(slabs // 2)]
                line = jnp.concatenate([held[i, orders, lanes] for i in bands], axis=1)
                name = (s * batch * chans + bc) * 2 + r
                for t, tile in enumerate(turned):
                    piece = line[:, t * LANES : min((t + 1) * LANES, depth)]
                    if piece.shape[1] < LANES:
                        blank = jnp.zeros((count, LANES - piece.shape[1]), jnp.float32)
                        piece = jnp.concatenate([piece, blank], axis=1)
                    tile[pl.ds(name, count, stride=names), :] = piece
    packed = packs(names, depth)

    def write(m, carry):
        rows = pl.ds(pl.multiple_of(m * names, names), names)
        for t, tile in enumerate(turned):
            block = tile[rows, :].astype(jnp.bfloat16)
            if packed and t == len(turned) - 1:
                step = names // 4
                last = block[3 * step :]
                for g in range(3):
                    both = jnp.concatenate(
                        [block[g * step : (g + 1) * step, :96], last[:, 32 * g : 32 * (g + 1)]], axis=1
                    )
                    out_ref[m, t * names + g * step : t * names + (g + 1) * step, :] = both
            else:
                out_ref[m, t * names : (t + 1) * names, :] = block
        return carry

    lax.fori_loop(0, count, write, 0)


def parity(blocks, sources, count, me, slabs, batch, chans, band, after):
    width = blocks[0].shape[2]
    names = 4 * batch * chans
    depth = band * slabs // 2
    total = packed_rows(names, depth)
    return pl.pallas_call(
        functools.partial(parity_kernel, slabs, sources, count, batch, chans, band),
        grid=(1,),
        in_specs=[pl.BlockSpec(memory_space=pltpu.SMEM)]
        + [pl.BlockSpec(block.shape, lambda g: (0, 0, 0)) for block in blocks]
        + [pl.BlockSpec(memory_space=pl.ANY)],
        out_specs=pl.BlockSpec((count, total, LANES), lambda g: (0, 0, 0)),
        out_shape=jax.ShapeDtypeStruct((count, total, LANES), jnp.bfloat16),
        scratch_shapes=[pltpu.VMEM((slabs, 2 * count, width), jnp.float32)]
        + [pltpu.VMEM((count * names, LANES), jnp.float32)] * -(-depth // LANES),
        compiler_params=pltpu.CompilerParams(vmem_limit_bytes=VMEM_LIMIT),
        cost_estimate=cost(count),
        name="parity",
    )(me, *blocks, after)


def project_kernel(groups, batch, first, info_ref, table_ref, *refs):
    parts, out_ref, rhs = refs[:groups], refs[-2], refs[-1]
    me, odd = info_ref[0], info_ref[1]
    orders, degrees, depth = table_ref.shape
    inner = rhs.shape[3]
    names = 2 * batch * inner
    packed = packs(names, depth)
    tiles = -(-depth // LANES)
    for m in range(orders):
        for d in range(groups):
            ch = me ^ d
            for sb in range(2 * batch):
                for t in range(tiles):
                    width = min(LANES, depth - t * LANES)
                    base = t * names
                    if packed and t == tiles - 1:
                        step = names // 4
                        if (sb + 1) * inner <= 3 * step:
                            block = parts[d][m, base + sb * inner : base + (sb + 1) * inner, :width]
                        else:
                            off = sb * inner - 3 * step
                            block = jnp.concatenate(
                                [
                                    parts[d][m, base + g * step + off : base + g * step + off + inner, 96:]
                                    for g in range(3)
                                ],
                                axis=1,
                            )
                    else:
                        block = parts[d][m, base + sb * inner : base + (sb + 1) * inner, :width]
                    rhs[m, sb, ch, :, t * LANES : t * LANES + width] = block
    row = lax.broadcasted_iota(jnp.int32, (degrees, batch * groups * inner), 0)
    start = pl.program_id(0) * orders + first
    for m in range(orders):
        right = rhs[m].reshape(2 * batch * groups * inner, depth)
        both = lax.dot_general(table_ref[m], right, NT, preferred_element_type=jnp.float32)
        cut = batch * groups * inner
        even = ((row + (odd + start + m)) & 1) == 0
        out_ref[m] = jnp.where(even, both[:, :cut], both[:, cut:])


def project(table, parts, starts, count, info, first, batch, inner, prior, after):
    slab, degrees, depth = table.shape
    groups = len(parts)
    total = parts[0].shape[1]
    step = 4 if count % 4 == 0 and first % 4 == 0 else count
    lead = first // step
    names = batch * groups * inner
    operands = [info, table, *parts]
    in_specs = [
        pl.BlockSpec(memory_space=pltpu.SMEM),
        pl.BlockSpec((step, degrees, depth), lambda g: (g + lead, 0, 0)),
    ] + [
        pl.BlockSpec((step, total, LANES), functools.partial(lambda skip, g: (g + skip, 0, 0), start // step))
        for start in starts
    ]
    aliases = {}
    if after is not None:
        operands.append(after)
        in_specs.append(pl.BlockSpec(memory_space=pl.ANY))
    if prior is not None:
        operands.append(prior)
        in_specs.append(pl.BlockSpec(memory_space=pl.ANY))
        aliases = {len(operands) - 1: 0}
    return pl.pallas_call(
        functools.partial(project_kernel, groups, batch, first),
        grid=(count // step,),
        in_specs=in_specs,
        out_specs=pl.BlockSpec((step, degrees, names), lambda g: (g + lead, 0, 0)),
        out_shape=jax.ShapeDtypeStruct((slab, degrees, names), jnp.float32),
        scratch_shapes=[pltpu.VMEM((step, 2 * batch, groups, inner, depth), jnp.bfloat16)],
        input_output_aliases=aliases,
        compiler_params=pltpu.CompilerParams(vmem_limit_bytes=VMEM_LIMIT),
        cost_estimate=cost(0),
        name="project",
    )(*operands)


def shards(slabs, groups, fields, table):
    batch, band, chans, nlon = fields.shape
    slab, degrees, depth = table.shape
    chips = slabs // 2
    lat, ch = lax.axis_index("lat").astype(jnp.int32), lax.axis_index("ch").astype(jnp.int32)
    me = lat.reshape(1)
    where = jnp.stack([lat % 2, lat // 2])
    south = (me >= chips).astype(jnp.int32)
    info = jnp.stack([ch, (ch * degrees + lat * slab) % 2])
    chunks = split_orders(slab)
    tables = [fourier_rows(nlon, slabs, slab, chunk) for chunk in chunks]
    bits = [1 << k for k in range(groups.bit_length() - 1)]

    def send(block, d):
        return lax.ppermute(block, "lat", xor_pairs(slabs, 2 * d))

    def pass_on(block, bit):
        return lax.ppermute(block, "ch", xor_pairs(groups, bit))

    own = reorder(fields, south)
    other = lax.ppermute(own, "lat", xor_pairs(slabs, 1))
    counts = [2 * count for _, count in chunks]
    total, out = len(chunks), None

    def orders(q, blocks, sources, after):
        return parity(blocks, tuple(sources), chunks[q][1], me, slabs, batch, chans, band, after)

    alone = tuple((d, 0, 1) for d in range(chips))
    near = dft([own], tables[0], counts[:1], alone, where, me, 0, 2)
    sends = dft([other], tables[0], counts[:1], alone, where, me, 1, 2, near)
    if groups != 4 or total != 3 or chips != 4:
        last = me
        for q, (first, count) in enumerate(chunks):
            if q:
                sends = dft([own, other], tables[q], counts[q : q + 1], alone, where, last)
            blocks = [sends[0]] + [send(sends[d], d) for d in range(1, chips)]
            last = orders(q, blocks, [(d, 0) for d in range(chips)], last)
            parts = [last]
            for bit in bits:
                parts += [pass_on(part, bit) for part in parts]
            out = project(table, parts, [0] * groups, count, info, first, batch, 2 * chans, out, last)
        return out

    layout = ((1, 0, 2),) + tuple((d, q, q + 1) for q in range(2) for d in (0, 2, 3))
    rest = dft([own, other], np.concatenate(tables[1:], axis=2), counts[1:], layout, where, sends[0])
    beside = send(rest[0], 1)
    later = [rest[1 + 3 * q : 4 + 3 * q] for q in range(2)]
    parts, pieces = {}, {}

    def spread(q, mine):
        if q == 2:
            (mine,) = gate([mine], [piece for _, _, piece in pieces[1]])
        parts[q] = {0: mine, 1: pass_on(mine, 1), 2: pass_on(mine, 2)}

    def forward(q, after):
        have, count = parts[q], chunks[q][1]
        sizes = [count - 16, 16] if q == 2 and count > 16 else [count]
        pieces[q] = []
        for begin, size in zip(np.cumsum([0] + sizes), sizes):
            lo, mid, hi = int(begin), int(begin) + size // 2, int(begin) + size
            held = gate([have[1][lo:mid], have[2][mid:hi]], [after])
            pieces[q] += [(lo, mid - lo, pass_on(held[0], 2)), (mid, hi - mid, pass_on(held[1], 1))]
            after = pieces[q][-1][2]
        return held[0]

    def finish(q, prior, after):
        for start, count, piece in pieces[q]:
            arrays = [parts[q][0], parts[q][1], parts[q][2], piece]
            begins = [start, start, start, 0]
            first = chunks[q][0] + start
            prior = project(table, arrays, begins, count, info, first, batch, 2 * chans, prior, after)
            after = None
        return prior

    def arrive(q, after):
        blocks = arrived[q]
        if q + 1 < total:
            stay, *leave = later[q]
            passed = [piece for _, _, piece in pieces.get(q - 1, [])]
            held = gate(leave, [*blocks[1:], *passed, after])
            arrived.append([stay, send(held[0], 2), send(held[1], 3)])
            after = held[0]
        if q == 0:
            mine = orders(q, blocks, [(d, 0) for d in range(4)], after)
        else:
            skip = sum(counts[1:q])
            mine = orders(q, [*blocks, beside], [(0, 0), (2, 0), (3, 0), (1, skip)], after)
        return mine

    arrived = [[sends[0]] + [send(sends[d], d) for d in range(1, 4)]]
    last = arrive(0, rest[0])
    spread(0, last)
    last = forward(0, last)
    last = arrive(1, last)
    spread(1, last)
    last = out = finish(0, out, last)
    mine = arrive(2, last)
    last = forward(1, mine)
    spread(2, mine)
    out = finish(1, out, last)
    forward(2, out)
    return finish(2, out, None)


def solution(mesh):
    return jax.shard_map(
        functools.partial(shards, mesh.shape["lat"], mesh.shape["ch"]),
        mesh=mesh,
        in_specs=(P(None, "lat", "ch", None), P("lat", "ch", None)),
        out_specs=P("lat", "ch", None),
        check_vma=False,
    )
```
